128 devices in a mesh: row: 8 (over y_hi, z), col: 16 (over y_lo, x, core).
Axes of the slice: x: 4, y: 4 (y_hi: 2, y_lo: 2; y = y_hi * 2 + y_lo), z: 4, core: 2. Of those that a mesh axis runs over, the one named last changes fastest.
Arguments:
- frames: bfloat16 [16, 256, 256, 128], P(None, 'row', 'col'), may hold values from -6 to 6
- cotangent: bfloat16 [16, 256, 256, 128], P(None, 'row', 'col'), may hold values from -6 to 6
- first_norm_gain: float32 [128], replicated, may hold values from 0.1 to 1.9
- w_qkv: bfloat16 [128, 384], replicated, may hold values from -0.5 to 0.5
- rel_bias: float32 [4, 256, 256], replicated, may hold values from -4 to 4
- w_proj: bfloat16 [128, 128], replicated, may hold values from -0.5 to 0.5
- second_norm_gain: float32 [128], replicated, may hold values from 0.1 to 1.9
- w_up: bfloat16 [128, 512], replicated, may hold values from -0.5 to 0.5
- w_down: bfloat16 [512, 128], replicated, may hold values from -0.25 to 0.25
Outputs:
- frames_input_gradient: float32 [16, 256, 256, 128], P(None, 'row', 'col')
- g_qkv: float32 [128, 384], replicated
- g_proj: float32 [128, 128], replicated
- g_up: float32 [128, 512], replicated
- g_down: float32 [512, 128], replicated
The draws below stay inside these ranges and needn't reach their ends.
All inputs are finite; a program needn't handle non-finite values.
Results may differ from the reference program's by a relative error of at most 0.015.
Values may be sent and summed in bfloat16 or wider, within the bound.
A program may use at most 192 MiB of HBM per device.

```python
import math
import jax
import jax.numpy as jnp
from jax import lax

D = 128
FF = 512
HEADS = 4
WS = 16
SHIFT = 8
FRAMES = 16
IMG_H = 256
IMG_W = 256


def steps_of(stream_key, dims, split, smallest, top_value):
    factor_of = 1.0
    for dim, parts in split:
        steps = jax.random.uniform(jax.random.fold_in(jax.random.fold_in(stream_key, 6), dim), (parts,), jnp.float32, smallest / len(split), top_value / len(split))
        factor_of = factor_of * jnp.repeat(jnp.exp(steps), dims[dim] // parts).reshape((-1,) + (1,) * (len(dims) - 1 - dim))
    return factor_of


def normal_values(key, dims, width, bound, shards=(), held_as=jnp.bfloat16):
    factor_of = steps_of(key, dims, shards, -0.22, 0.18) if shards else 1.0
    values = jax.random.normal(key, dims, jnp.float32) * width * factor_of
    return jnp.minimum(jnp.maximum(values, -bound), bound).astype(held_as)


def setup_inputs(seed: int = 0) -> dict:
    arg_keys = jax.random.split(jax.random.key(seed), 10)
    return {
        "frames": normal_values(arg_keys[0], (FRAMES, IMG_H, IMG_W, D), 1.0, 6.0, ((1, 8), (2, 16))),
        "cotangent": normal_values(arg_keys[1], (FRAMES, IMG_H, IMG_W, D), 1.0, 6.0, ((1, 8), (2, 16))),
        "first_norm_gain": jnp.clip(1.0 + 0.18 * jax.random.normal(arg_keys[2], (D,), jnp.float32), 0.1, 1.9),
        "w_qkv": normal_values(arg_keys[3], (D, 3 * D), D ** -0.5, 0.5),
        "rel_bias": normal_values(arg_keys[4], (HEADS, WS * WS, WS * WS), 1.0, 4.0, (), jnp.float32),
        "w_proj": normal_values(arg_keys[5], (D, D), D ** -0.5, 0.5),
        "second_norm_gain": jnp.clip(1.0 + 0.18 * jax.random.normal(arg_keys[6], (D,), jnp.float32), 0.1, 1.9),
        "w_up": normal_values(arg_keys[7], (D, FF), D ** -0.5, 0.5),
        "w_down": normal_values(arg_keys[8], (FF, D), FF ** -0.5, 0.25),
    }


EPS = 1e-05

def layer_norm_forward(x, norm_gain_vector):
    xf = x.astype(jnp.float32)
    centered_values = xf - lax.optimization_barrier(jnp.mean(xf, -1, keepdims=True))
    inverse_deviation = lax.rsqrt(lax.optimization_barrier(jnp.mean(centered_values * centered_values, -1, keepdims=True)) + EPS)
    normalized_input = centered_values * inverse_deviation
    return (normalized_input * norm_gain_vector, normalized_input, inverse_deviation)

def layer_norm_backward(upstream_gradient, norm_gain_vector, normalized_input, inverse_deviation):
    normalized_gradient = upstream_gradient * norm_gain_vector
    return inverse_deviation * (normalized_gradient - lax.optimization_barrier(jnp.mean(normalized_gradient, -1, keepdims=True)) - normalized_input * lax.optimization_barrier(jnp.mean(normalized_gradient * normalized_input, -1, keepdims=True)))

def split_windows(t, ws):
    f, h, w, c = t.shape
    t = t.reshape(f, h // ws, ws, w // ws, ws, c).transpose(0, 1, 3, 2, 4, 5)
    return t.reshape(f * (h // ws) * (w // ws), ws * ws, c)

def merge_windows(t, f, h, w, ws):
    c = t.shape[-1]
    t = t.reshape(f, h // ws, w // ws, ws, ws, c).transpose(0, 1, 3, 2, 4, 5)
    return t.reshape(f, h, w, c)

def regions(start, count, total, ws, sh):
    pos = start + jnp.arange(count, dtype=jnp.int32)
    return jnp.where(pos < total - ws, 0, jnp.where(pos < total - sh, 1, 2)).astype(jnp.int32)

def gelu_parts(u):
    cdf = 0.5 * (1.0 + jax.scipy.special.erf(u * (1.0 / math.sqrt(2.0))))
    dens = jnp.exp(-0.5 * u * u) * (1.0 / math.sqrt(2.0 * math.pi))
    return (u * cdf, cdf + u * dens)

def probabilities(qkv, labels, rel_bias, heads):
    b, l, c3 = qkv.shape
    c = c3 // 3
    hd = c // heads
    query = qkv[..., :c].reshape(b, l, heads, hd)
    keys = qkv[..., c:2 * c].reshape(b, l, heads, hd)
    values = qkv[..., 2 * c:].reshape(b, l, heads, hd)
    scores = jnp.einsum('blhd,bmhd->bhlm', query.astype(jnp.float32), keys.astype(jnp.float32)) * hd ** (-0.5)
    mask = jnp.where(labels[:, :, None] == labels[:, None, :], 0.0, -100.0).astype(jnp.float32)
    scores = scores + rel_bias[None] + mask[:, None]
    scores = scores - lax.optimization_barrier(jnp.max(scores, -1, keepdims=True))
    expo = jnp.exp(scores)
    probs = expo / lax.optimization_barrier(jnp.sum(expo, -1, keepdims=True))
    return (query, keys, values, probs)

def attend_fwd(qkv, labels, rel_bias, heads):
    b, l, c3 = qkv.shape
    query, keys, values, probs = probabilities(qkv, labels, rel_bias, heads)
    probs_b = probs.astype(jnp.bfloat16)
    out = jnp.einsum('bhlm,bmhd->blhd', probs_b.astype(jnp.float32), values.astype(jnp.float32))
    return out.astype(jnp.bfloat16).reshape(b, l, c3 // 3)

def attend_bwd(qkv, labels, rel_bias, grad_out, heads):
    b, l, c3 = qkv.shape
    c = c3 // 3
    hd = c // heads
    query, keys, values, probs = probabilities(qkv, labels, rel_bias, heads)
    probs_b = probs.astype(jnp.bfloat16).astype(jnp.float32)
    grad_heads = grad_out.reshape(b, l, heads, hd).astype(jnp.float32)
    d_val = jnp.einsum('bhlm,blhd->bmhd', probs_b, grad_heads).astype(jnp.bfloat16)
    d_prob = jnp.einsum('blhd,bmhd->bhlm', grad_heads, values.astype(jnp.float32))
    d_score = probs * (d_prob - lax.optimization_barrier(jnp.sum(d_prob * probs, -1, keepdims=True)))
    d_score = (d_score * hd ** (-0.5)).astype(jnp.bfloat16).astype(jnp.float32)
    d_query = jnp.einsum('bhlm,bmhd->blhd', d_score, keys.astype(jnp.float32)).astype(jnp.bfloat16)
    d_key = jnp.einsum('bhlm,blhd->bmhd', d_score, query.astype(jnp.float32)).astype(jnp.bfloat16)
    return jnp.concatenate([d_query.reshape(b, l, c), d_key.reshape(b, l, c), d_val.reshape(b, l, c)], -1)

def blocked(func, arrays, per):
    count = arrays[0].shape[0]
    grouped = tuple((a.reshape((count // per, per) + a.shape[1:]) for a in arrays))
    result = lax.map(lambda items: func(*items), grouped)
    return result.reshape((count,) + result.shape[2:])

def reference(frames, cotangent, first_norm_gain, w_qkv, rel_bias, w_proj, second_norm_gain, w_up, w_down):
    nfr, hgt, wid, chan = frames.shape
    attention_residual_output, first_normalized_input, first_inverse_deviation = layer_norm_forward(frames, first_norm_gain)
    y_b = attention_residual_output.astype(jnp.bfloat16)
    shifted = split_windows(jnp.roll(y_b, (-SHIFT, -SHIFT), (1, 2)), WS)
    nwin, length, _ = shifted.shape
    flat_in = shifted.reshape(-1, chan)
    qkv = jnp.dot(flat_in, w_qkv, preferred_element_type=jnp.float32).astype(jnp.bfloat16).reshape(nwin, length, 3 * chan)
    grid = regions(0, hgt, hgt, WS, SHIFT)[:, None] * 3 + regions(0, wid, wid, WS, SHIFT)[None, :]
    labels = split_windows(jnp.broadcast_to(grid[None, :, :, None], (nfr, hgt, wid, 1)), WS)[..., 0]
    per = math.gcd(nwin, max(1, 2048 // length))
    attended = blocked(lambda a, b: attend_fwd(a, b, rel_bias, HEADS), (qkv, labels), per).reshape(-1, chan)
    proj = jnp.dot(attended, w_proj, preferred_element_type=jnp.float32).astype(jnp.bfloat16)
    proj = jnp.roll(merge_windows(proj.reshape(nwin, length, chan), nfr, hgt, wid, WS), (SHIFT, SHIFT), (1, 2))
    first_residual_input = (frames.astype(jnp.float32) + proj.astype(jnp.float32)).astype(jnp.bfloat16)
    block_final_output, second_normalized_input, second_inverse_deviation = layer_norm_forward(first_residual_input, second_norm_gain)
    z_b = block_final_output.astype(jnp.bfloat16).reshape(-1, chan)
    u_pre = jnp.dot(z_b, w_up, preferred_element_type=jnp.float32)
    act, slope = gelu_parts(u_pre)
    hid = act.astype(jnp.bfloat16)
    upstream_gradient = cotangent.reshape(-1, chan)
    g_down = jnp.dot(hid.T, upstream_gradient, preferred_element_type=jnp.float32)
    d_hid = jnp.dot(upstream_gradient, w_down.T, preferred_element_type=jnp.float32)
    d_up = (d_hid * slope).astype(jnp.bfloat16)
    g_up = jnp.dot(z_b.T, d_up, preferred_element_type=jnp.float32)
    residual_gradient = jnp.dot(d_up, w_up.T, preferred_element_type=jnp.float32).reshape(frames.shape)
    first_residual_gradient = cotangent.astype(jnp.float32) + layer_norm_backward(residual_gradient, second_norm_gain, second_normalized_input, second_inverse_deviation)
    dx_b = first_residual_gradient.astype(jnp.bfloat16)
    d_win = split_windows(jnp.roll(dx_b, (-SHIFT, -SHIFT), (1, 2)), WS).reshape(-1, chan)
    g_proj = jnp.dot(attended.T, d_win, preferred_element_type=jnp.float32)
    d_att = jnp.dot(d_win, w_proj.T, preferred_element_type=jnp.float32).astype(jnp.bfloat16).reshape(nwin, length, chan)
    d_qkv = blocked(lambda a, b, d: attend_bwd(a, b, rel_bias, d, HEADS), (qkv, labels, d_att), per).reshape(-1, 3 * chan)
    g_qkv = jnp.dot(flat_in.T, d_qkv, preferred_element_type=jnp.float32)
    shifted_gradient = jnp.dot(d_qkv, w_qkv.T, preferred_element_type=jnp.float32).astype(jnp.bfloat16)
    shifted_gradient = jnp.roll(merge_windows(shifted_gradient.reshape(nwin, length, chan), nfr, hgt, wid, WS), (SHIFT, SHIFT), (1, 2))
    frames_input_gradient = first_residual_gradient + layer_norm_backward(shifted_gradient.astype(jnp.float32), first_norm_gain, first_normalized_input, first_inverse_deviation)
    factor = float(nfr * hgt * wid) ** (-0.5)
    return (frames_input_gradient, g_qkv * factor, g_proj * factor, g_up * factor, g_down * factor)
```

```python
import functools
import math

import jax
import jax.numpy as jnp
from jax import lax
from jax.experimental import pallas as pl
from jax.experimental.pallas import tpu as pltpu
from jax.sharding import PartitionSpec as P

HEADS = 4
WS = 16
SHIFT = 8
EPS = 1e-05
LOG2E = math.log2(math.e)
MESH = pl.DeviceIdType.MESH
bf16 = jnp.bfloat16
f32 = jnp.float32


def dot(a, b, ca, cb):
    return lax.dot_general(a, b, (((ca,), (cb,)), ((), ())), preferred_element_type=f32)


def layer_norm_stats(x):
    centered = x - jnp.mean(x, -1, keepdims=True)
    rstd = lax.rsqrt(jnp.mean(centered * centered, -1, keepdims=True) + EPS)
    return centered * rstd, rstd


def layer_norm_backward(dy, gain, xhat, rstd):
    dxh = dy * gain
    return rstd * (
        dxh
        - jnp.mean(dxh, -1, keepdims=True)
        - xhat * jnp.mean(dxh * xhat, -1, keepdims=True)
    )


def gelu_and_slope(u):
    expo = jnp.exp2(u * u * (-0.5 * LOG2E))
    t = 1.0 / (1.0 + (0.3275911 / math.sqrt(2.0)) * jnp.abs(u))
    poly = 0.5 * 1.061405429
    for c in (-1.453152027, 1.421413741, -0.284496736, 0.254829592):
        poly = t * poly + 0.5 * c
    tail = t * poly * expo
    cdf = jnp.where(u < 0.0, tail, 1.0 - tail)
    return u * cdf, cdf + u * expo * (1.0 / math.sqrt(2.0 * math.pi))


def window_block(x, c, w, g1, g2, w_qkv, w_proj, w_up, w_down, bias, probs, acc):
    gq, gp, gu, gd = acc
    tokens, chan = x.shape
    hd = chan // HEADS
    head = lax.broadcasted_iota(jnp.int32, (tokens, chan), 1) // hd
    xhat1, rstd1 = layer_norm_stats(x)
    y = (xhat1 * g1).astype(bf16)
    qkv = dot(y, w_qkv[...], 1, 0)
    q = qkv[:, :chan] * (LOG2E / math.sqrt(hd))
    k = qkv[:, chan : 2 * chan].astype(bf16)
    v_one = jnp.concatenate([qkv[:, 2 * chan :].astype(bf16), jnp.ones((tokens, chan), bf16)], 1)
    total, norm = None, None
    for h in range(HEADS):
        mine = head == h
        scores = dot(jnp.where(mine, q, 0.0).astype(bf16), k, 1, 1) + bias[w, h]
        expo = jnp.exp2(scores - jnp.max(scores, -1, keepdims=True)).astype(bf16)
        probs[w, h] = expo
        out = dot(expo, v_one, 1, 0)
        total = out[:, :chan] if h == 0 else jnp.where(mine, out[:, :chan], total)
        norm = out[:, chan:] if h == 0 else jnp.where(mine, out[:, chan:], norm)
    inverse = 1.0 / norm
    attended = total * inverse
    attended_b = attended.astype(bf16)
    proj = dot(attended_b, w_proj[...], 1, 0).astype(bf16)
    x1 = (x + proj.astype(f32)).astype(bf16).astype(f32)
    xhat2, rstd2 = layer_norm_stats(x1)
    z = (xhat2 * g2).astype(bf16)
    c_b = c.astype(bf16)
    act, slope = gelu_and_slope(dot(z, w_up[...], 1, 0))
    hid = act.astype(bf16)
    du = (dot(c_b, w_down[...], 1, 1) * slope).astype(bf16)
    gd[...] += dot(c_b, hid, 0, 0)
    gu[...] += dot(z, du, 0, 0)
    dx1 = c + layer_norm_backward(dot(du, w_up[...], 1, 1), g2, xhat2, rstd2)
    dx1_b = dx1.astype(bf16)
    gp[...] += dot(attended_b, dx1_b, 0, 0)
    d_att = dot(dx1_b, w_proj[...], 1, 1).astype(bf16).astype(f32) * inverse
    d_sum = -(d_att * attended)
    q_t = q.astype(bf16).T
    d_att_t = d_att.astype(bf16).T
    dv, dk, dq = [], [], None
    for h in range(HEADS):
        mine = head == h
        left = jnp.concatenate(
            [jnp.where(mine, d_att, 0.0).astype(bf16), jnp.where(mine, d_sum, 0.0).astype(bf16)], 1
        )
        expo = probs[w, h]
        ds = (expo.astype(f32) * dot(left, v_one, 1, 1)).astype(bf16)
        dv.append(dot(d_att_t[hd * h : hd * (h + 1)], expo, 1, 0))
        dk.append(dot(q_t[hd * h : hd * (h + 1)], ds, 1, 0))
        out = dot(ds, k, 1, 0)
        dq = out if h == 0 else jnp.where(mine, out, dq)
    dqkv = jnp.concatenate(
        [
            (dq * hd**-0.5).astype(bf16),
            (jnp.concatenate(dk, 0) * (1.0 / LOG2E)).astype(bf16).T,
            jnp.concatenate(dv, 0).astype(bf16).T,
        ],
        1,
    )
    gq[...] += dot(y, dqkv, 0, 0)
    d_shift = dot(dqkv, w_qkv[...], 1, 1).astype(bf16).astype(f32)
    return dx1 + layer_norm_backward(d_shift, g1, xhat1, rstd1)


def halves(tile):
    return tile.reshape(tile.shape[0] // 2, 2 * tile.shape[1], tile.shape[2]).astype(bf16)


def unhalves(packed):
    return packed.astype(f32).reshape(packed.shape[0] * 2, packed.shape[1] // 2, packed.shape[2])


def block_kernel(
    n_row, n_col, factor,
    frames, cotangent, gain1, w_qkv, rel_bias, w_proj, gain2, w_up, w_down,
    grad, g_qkv, g_proj, g_up, g_down,
    to_left, to_up, to_diag, from_right, from_down, from_diag,
    to_right, to_down, to_diag2, from_left, from_up, from_diag2,
    tile, probs, bias, gq, gp, gu, gd,
    red, red_send, red_core, red_x, red_z, red_y, full,
    in_send, in_recv, out_send, out_recv, grad_sem, red_ssem, red_rsem,
):
    nfr, tile_h, tile_w, chan = frames.shape
    row, col = lax.axis_index("row"), lax.axis_index("col")
    n_z = min(4, n_row)
    n_yh = n_row // n_z
    n_x = min(4, n_col // 2)
    n_yl = n_col // (2 * n_x)
    n_y = n_yh * n_yl
    core, x_at, y_lo = lax.rem(col, 2), lax.rem(col // 2, n_x), col // (2 * n_x)
    z_at, y_hi = lax.rem(row, n_z), row // n_z
    y_at = y_hi * n_yl + y_lo

    left, right = lax.rem(col + n_col - 1, n_col), lax.rem(col + 1, n_col)
    up, down = lax.rem(row + n_row - 1, n_row), lax.rem(row + 1, n_row)
    in_to = ((row, left), (up, col), (up, left))
    out_to = ((row, right), (down, col), (down, right))

    def core_peer(s):
        return (row, col + 1 - 2 * core)

    def x_peer(s):
        return (row, (y_lo * n_x + lax.rem(x_at + s, n_x)) * 2 + core)

    def z_peer(s):
        return (y_hi * n_z + lax.rem(z_at + s, n_z), col)

    def y_peer(s):
        other = lax.rem(y_at + s, n_y)
        return ((other // n_yl) * n_z + z_at, (lax.rem(other, n_yl) * n_x + x_at) * 2 + core)

    peers = list(in_to) + list(out_to) + [core_peer(1)]
    peers += [x_peer(s) for s in range(1, n_x)]
    peers += [z_peer(s) for s in range(1, n_z)]
    peers += [y_peer(s) for s in range(1, n_y)]
    barrier = pltpu.get_barrier_semaphore()
    for peer in peers:
        pl.semaphore_signal(barrier, inc=1, device_id=peer, device_id_type=MESH)
    pl.semaphore_wait(barrier, len(peers))

    def in_copies(f):
        pairs = ((to_left, from_right), (to_up, from_down), (to_diag, from_diag))
        return [
            pltpu.make_async_remote_copy(
                src_ref=a.at[f], dst_ref=b.at[f],
                send_sem=in_send.at[i, f], recv_sem=in_recv.at[i, f],
                device_id=in_to[i], device_id_type=MESH,
            )
            for i, (a, b) in enumerate(pairs)
        ]

    def out_copies(f):
        pairs = ((to_right, from_left), (to_down, from_up), (to_diag2, from_diag2))
        return [
            pltpu.make_async_remote_copy(
                src_ref=a.at[f], dst_ref=b.at[f],
                send_sem=out_send.at[i, f], recv_sem=out_recv.at[i, f],
                device_id=out_to[i], device_id_type=MESH,
            )
            for i, (a, b) in enumerate(pairs)
        ]

    def send_in(f):
        for i, source in enumerate((frames, cotangent)):
            whole = source[f].astype(f32)
            to_left[f, i] = halves(whole[SHIFT:, :SHIFT])
            to_up[f, i] = halves(whole[:SHIFT, SHIFT:])
            to_diag[f, i] = halves(whole[:SHIFT, :SHIFT])
        for copy in in_copies(f):
            copy.start()

    def grad_copy(f):
        return pltpu.make_async_copy(tile.at[f], grad.at[f], grad_sem.at[f])

    def finish(f):
        for copy in out_copies(f):
            copy.wait_recv()
        tile[f, SHIFT:, :SHIFT] = unhalves(from_left[f])
        tile[f, :SHIFT, SHIFT:] = unhalves(from_up[f])
        tile[f, :SHIFT, :SHIFT] = unhalves(from_diag2[f])
        grad_copy(f).start()

    ahead = min(3, nfr)
    for f in range(ahead):
        send_in(f)

    wide = WS * WS
    at_q = lax.broadcasted_iota(jnp.int32, (wide, wide), 0)
    at_k = lax.broadcasted_iota(jnp.int32, (wide, wide), 1)
    cut_row = (at_q // (WS * SHIFT)) != (at_k // (WS * SHIFT))
    cut_col = (lax.rem(at_q, WS) // SHIFT) != (lax.rem(at_k, WS) // SHIFT)
    last_row = jnp.where(row == n_row - 1, 1.0, 0.0)
    last_col = jnp.where(col == n_col - 1, 1.0, 0.0)
    by_row = jnp.where(cut_row, last_row, 0.0)
    by_col = jnp.where(cut_col, last_col, 0.0)
    windows = tile_h // WS
    for w in range(windows):
        cut = jnp.maximum(by_row, by_col) if w == windows - 1 else by_col
        for h in range(HEADS):
            bias[w, h] = (rel_bias[h] + cut * -100.0) * LOG2E
    for ref in (gq, gp, gu, gd):
        ref[...] = jnp.zeros_like(ref)

    def frame_step(f, carry):
        @pl.when(f + ahead < nfr)
        def _():
            send_in(f + ahead)

        for copy in in_copies(f):
            copy.wait_recv()
        parts = []
        for i, source in enumerate((frames, cotangent)):
            own = source[f].astype(f32)[SHIFT:, SHIFT:]
            first = jnp.concatenate([own, unhalves(from_down[f, i])], 0)
            second = jnp.concatenate([unhalves(from_right[f, i]), unhalves(from_diag[f, i])], 0)
            shifted = jnp.concatenate([first, second], 1)
            parts.append(
                [shifted[w * WS : (w + 1) * WS].reshape(wide, chan) for w in range(windows)]
            )
        result = []
        for w in range(windows):
            out = window_block(
                parts[0][w], parts[1][w], w, gain1[...], gain2[...], w_qkv, w_proj, w_up, w_down,
                bias, probs, (gq, gp, gu, gd),
            )
            result.append(out.reshape(WS, WS, chan))
        out = jnp.concatenate(result, 0)
        keep = tile_h - SHIFT
        to_right[f] = halves(out[:keep, SHIFT:])
        to_down[f] = halves(out[keep:, :SHIFT])
        to_diag2[f] = halves(out[keep:, SHIFT:])
        for copy in out_copies(f):
            copy.start()
        tile[f, SHIFT:, SHIFT:] = out[:keep, :SHIFT]

        @pl.when(f >= 2)
        def _():
            finish(f - 2)

        return carry

    lax.fori_loop(0, nfr, frame_step, 0)

    for j in range(3):
        red[chan * j : chan * (j + 1)] = gq[:, chan * j : chan * (j + 1)]
    red[3 * chan : 4 * chan] = gp[...]
    for j in range(4):
        red[chan * (4 + j) : chan * (5 + j)] = gu[:, chan * j : chan * (j + 1)]
        red[chan * (8 + j) : chan * (9 + j)] = gd[:, chan * j : chan * (j + 1)]
    rows = red.shape[0]
    size_c = rows // 2
    size_x = size_c // n_x
    size_z = size_x // n_z

    def copy_to(peer, src, dst, sem):
        return pltpu.make_async_remote_copy(
            src_ref=src, dst_ref=dst, send_sem=red_ssem.at[sem], recv_sem=red_rsem.at[sem],
            device_id=peer, device_id_type=MESH,
        )

    def at(start, size):
        return pl.ds(pl.multiple_of(start, 16), size)

    red_send[...] = red[...].astype(bf16)
    sem = 0
    copies = []
    base = core * size_c
    first = copy_to(core_peer(1), red_send.at[at((1 - core) * size_c, size_c)], red_core, sem)
    first.start()
    copies.append(first)
    sem += 1
    for f in range(max(nfr - 2, 0), nfr):
        finish(f)
    first.wait_recv()
    red[at(base, size_c)] += red_core[...].astype(f32)

    def reduce_stage(base, size, n, index, peer, landing, sem):
        red_send2 = red_stage[len(landings)]
        landings.append(0)
        red_send2[...] = red[at(base, size * n)].astype(bf16)
        started = []
        for s in range(1, n):
            other = lax.rem(index + s, n)
            started.append(
                copy_to(peer(s), red_send2.at[at(other * size, size)], landing.at[s - 1], sem)
            )
            started[-1].start()
            sem += 1
        base = base + index * size
        for copy in started:
            copy.wait_recv()
        total = red[at(base, size)]
        for s in range(1, n):
            total += landing[s - 1].astype(f32)
        red[at(base, size)] = total
        copies.extend(started)
        return base, sem

    landings = []
    red_stage = (full.at[pl.ds(rows, size_c)], full.at[pl.ds(rows + size_c, size_x)])
    base, sem = reduce_stage(base, size_x, n_x, x_at, x_peer, red_x, sem)
    base, sem = reduce_stage(base, size_z, n_z, z_at, z_peer, red_z, sem)
    red_y[y_at] = red[at(base, size_z)].astype(bf16)
    started = []
    for s in range(1, n_y):
        started.append(copy_to(y_peer(s), red_y.at[y_at], red_y.at[y_at], sem))
        started[-1].start()
        sem += 1
    for copy in started:
        copy.wait_recv()
    copies.extend(started)
    total = red_y[0].astype(f32)
    for j in range(1, n_y):
        total += red_y[j].astype(f32)
    full[at(base, size_z)] = total.astype(bf16)

    def gather_stage(base, size, n, peer, sem):
        started = []
        for s in range(1, n):
            part = full.at[at(base, size)]
            started.append(copy_to(peer(s), part, part, sem))
            started[-1].start()
            sem += 1
        for copy in started:
            copy.wait_recv()
        copies.extend(started)
        return sem

    sem = gather_stage(base, size_z, n_z, z_peer, sem)
    sem = gather_stage(core * size_c + x_at * size_x, size_x, n_x, x_peer, sem)
    sem = gather_stage(core * size_c, size_c, 2, core_peer, sem)
    for j in range(3):
        g_qkv[:, chan * j : chan * (j + 1)] = (
            full[chan * j : chan * (j + 1)].astype(f32) * factor
        )
    g_proj[...] = full[3 * chan : 4 * chan].astype(f32) * factor
    for j in range(4):
        g_up[:, chan * j : chan * (j + 1)] = (
            full[chan * (4 + j) : chan * (5 + j)].astype(f32) * factor
        )
        g_down[chan * j : chan * (j + 1)] = (
            full[chan * (8 + j) : chan * (9 + j)].astype(f32) * factor
        ).T
    for copy in copies:
        copy.wait_send()

    def drain(f, carry):
        for copy in in_copies(f) + out_copies(f):
            copy.wait_send()
        grad_copy(f).wait()
        return carry

    lax.fori_loop(0, nfr, drain, 0)


def solution(mesh):
    n_row, n_col = mesh.shape["row"], mesh.shape["col"]

    def shards(frames, cotangent, gain1, w_qkv, rel_bias, w_proj, gain2, w_up, w_down):
        nfr, tile_h, tile_w, chan = frames.shape
        ff = w_up.shape[1]
        factor = float(nfr * tile_h * tile_w * n_row * n_col) ** -0.5
        long, short = (tile_h - SHIFT) // 2, SHIFT // 2
        wide = WS * WS
        rows = 4 * chan + 2 * ff
        n_z, n_x = min(4, n_row), min(4, n_col // 2)
        n_y = (n_row // n_z) * (n_col // (2 * n_x))
        size_c = rows // 2
        size_x = size_c // n_x
        size_z = size_x // n_z
        n_sem = 2 + 2 * (n_x - 1) + 2 * (n_z - 1) + (n_y - 1)

        def pieces(k):
            sizes = (long, short, short)
            lead = (nfr,) if k == 1 else (nfr, k)
            return [pltpu.VMEM(lead + (s, 2 * SHIFT, chan), bf16) for s in sizes]

        vmem = pl.BlockSpec(memory_space=pltpu.VMEM)
        return pl.pallas_call(
            functools.partial(block_kernel, n_row, n_col, factor),
            out_shape=[
                jax.ShapeDtypeStruct(frames.shape, f32),
                jax.ShapeDtypeStruct((chan, 3 * chan), f32),
                jax.ShapeDtypeStruct((chan, chan), f32),
                jax.ShapeDtypeStruct((chan, ff), f32),
                jax.ShapeDtypeStruct((ff, chan), f32),
            ],
            in_specs=[vmem] * 9,
            out_specs=[pl.BlockSpec(memory_space=pl.ANY)] + [vmem] * 4,
            scratch_shapes=pieces(2) + pieces(2) + pieces(1) + pieces(1)
            + [
                pltpu.VMEM(frames.shape, f32),
                pltpu.VMEM((tile_h // WS, HEADS, wide, wide), bf16),
                pltpu.VMEM((tile_h // WS, HEADS, wide, wide), f32),
                pltpu.VMEM((chan, 3 * chan), f32),
                pltpu.VMEM((chan, chan), f32),
                pltpu.VMEM((chan, ff), f32),
                pltpu.VMEM((chan, ff), f32),
                pltpu.VMEM((rows, chan), f32),
                pltpu.VMEM((rows, chan), bf16),
                pltpu.VMEM((size_c, chan), bf16),
                pltpu.VMEM((max(n_x - 1, 1), size_x, chan), bf16),
                pltpu.VMEM((max(n_z - 1, 1), size_z, chan), bf16),
                pltpu.VMEM((n_y, size_z, chan), bf16),
                pltpu.VMEM((rows + size_c + size_x, chan), bf16),
                pltpu.SemaphoreType.DMA((3, nfr)),
                pltpu.SemaphoreType.DMA((3, nfr)),
                pltpu.SemaphoreType.DMA((3, nfr)),
                pltpu.SemaphoreType.DMA((3, nfr)),
                pltpu.SemaphoreType.DMA((nfr,)),
                pltpu.SemaphoreType.DMA((n_sem,)),
                pltpu.SemaphoreType.DMA((n_sem,)),
            ],
            compiler_params=pltpu.CompilerParams(
                collective_id=0, has_side_effects=True, vmem_limit_bytes=56 * 2**20
            ),
        )(
            frames, cotangent, gain1.reshape(1, chan), w_qkv, rel_bias, w_proj,
            gain2.reshape(1, chan), w_up, w_down,
        )

    tiles = P(None, "row", "col", None)
    return jax.shard_map(
        shards,
        mesh=mesh,
        in_specs=(tiles, tiles) + (P(),) * 7,
        out_specs=(tiles, P(), P(), P(), P()),
        check_vma=False,
    )
```

```python
import functools
import math

import jax
import jax.numpy as jnp
from jax import lax
from jax.experimental import pallas as pl
from jax.experimental.pallas import tpu as pltpu
from jax.sharding import PartitionSpec as P

HEADS = 4
WS = 16
SHIFT = 8
EPS = 1e-05
LOG2E = math.log2(math.e)
MESH = pl.DeviceIdType.MESH
bf16 = jnp.bfloat16
f32 = jnp.float32
PER = 2


def dot(a, b, ca, cb):
    return lax.dot_general(a, b, (((ca,), (cb,)), ((), ())), preferred_element_type=f32)


def layer_norm_stats(x):
    centered = x - jnp.mean(x, -1, keepdims=True)
    rstd = lax.rsqrt(jnp.mean(centered * centered, -1, keepdims=True) + EPS)
    return centered * rstd, rstd


def layer_norm_backward(dy, gain, xhat, rstd):
    dxh = dy * gain
    return rstd * (
        dxh
        - jnp.mean(dxh, -1, keepdims=True)
        - xhat * jnp.mean(dxh * xhat, -1, keepdims=True)
    )


def gelu_and_slope(u):
    expo = jnp.exp2(u * u * (-0.5 * LOG2E))
    t = 1.0 / (1.0 + (0.3275911 / math.sqrt(2.0)) * jnp.abs(u))
    poly = 0.5 * 1.061405429
    for c in (-1.453152027, 1.421413741, -0.284496736, 0.254829592):
        poly = t * poly + 0.5 * c
    tail = t * poly * expo
    cdf = jnp.where(u < 0.0, tail, 1.0 - tail)
    return u * cdf, cdf + u * expo * (1.0 / math.sqrt(2.0 * math.pi))


def window_block(at, x, c, bias, g1, g2, w_qkv, w_proj, w_up, w_down, probs, acc, result):
    gq, gp, gu, gd = acc
    tokens, chan = x.shape
    hd = chan // HEADS
    ff = w_up.shape[1]
    head = lax.broadcasted_iota(jnp.int32, (tokens, chan), 1) // hd
    xhat1, rstd1 = layer_norm_stats(x)
    y = (xhat1 * g1).astype(bf16)
    yield
    qkv = dot(y, w_qkv[...], 1, 0)
    yield
    q = qkv[:, :chan] * (LOG2E / math.sqrt(hd))
    k = qkv[:, chan : 2 * chan].astype(bf16)
    v_one = jnp.concatenate([qkv[:, 2 * chan :].astype(bf16), jnp.ones((tokens, chan), bf16)], 1)
    yield
    total, norm = None, None
    for h in range(HEADS):
        mine = head == h
        scores = dot(jnp.where(mine, q, 0.0).astype(bf16), k, 1, 1) + bias[h]
        yield
        expo = jnp.exp2(scores - jnp.max(scores, -1, keepdims=True)).astype(bf16)
        probs[at, h] = expo
        yield
        out = dot(expo, v_one, 1, 0)
        total = out[:, :chan] if h == 0 else jnp.where(mine, out[:, :chan], total)
        norm = out[:, chan:] if h == 0 else jnp.where(mine, out[:, chan:], norm)
        yield
    inverse = 1.0 / norm
    attended = total * inverse
    attended_b = attended.astype(bf16)
    proj = dot(attended_b, w_proj[...], 1, 0).astype(bf16)
    yield
    x1 = (x + proj.astype(f32)).astype(bf16).astype(f32)
    xhat2, rstd2 = layer_norm_stats(x1)
    z = (xhat2 * g2).astype(bf16)
    c_b = c.astype(bf16)
    yield
    z_t, c_t = z.T, c_b.T
    dz = None
    part = ff // 2
    for j in range(0, ff, part):
        u = dot(z, w_up[:, j : j + part], 1, 0)
        d_hid = dot(c_b, w_down[j : j + part, :], 1, 1)
        yield
        act, slope = gelu_and_slope(u)
        hid = act.astype(bf16)
        du = (d_hid * slope).astype(bf16)
        yield
        gd[:, j : j + part] += dot(c_t, hid, 1, 0)
        gu[:, j : j + part] += dot(z_t, du, 1, 0)
        more = dot(du, w_up[:, j : j + part], 1, 1)
        dz = more if dz is None else dz + more
        yield
    dx1 = c + layer_norm_backward(dz, g2, xhat2, rstd2)
    dx1_b = dx1.astype(bf16)
    gp[...] += dot(attended_b, dx1_b, 0, 0)
    d_att = dot(dx1_b, w_proj[...], 1, 1).astype(bf16).astype(f32)
    yield
    d_att = d_att * inverse
    d_sum = -(d_att * attended)
    q_t = q.astype(bf16).T
    d_att_t = d_att.astype(bf16).T
    yield
    dv, dk, dq = [], [], None
    for h in range(HEADS):
        mine = head == h
        left = jnp.concatenate(
            [jnp.where(mine, d_att, 0.0).astype(bf16), jnp.where(mine, d_sum, 0.0).astype(bf16)], 1
        )
        d_prob = dot(left, v_one, 1, 1)
        yield
        expo = probs[at, h]
        ds = (expo.astype(f32) * d_prob).astype(bf16)
        yield
        dv.append(dot(d_att_t[hd * h : hd * (h + 1)], expo, 1, 0))
        dk.append(dot(q_t[hd * h : hd * (h + 1)], ds, 1, 0))
        out = dot(ds, k, 1, 0)
        dq = out if h == 0 else jnp.where(mine, out, dq)
        yield
    dqkv = jnp.concatenate(
        [
            (dq * hd**-0.5).astype(bf16),
            (jnp.concatenate(dk, 0) * (1.0 / LOG2E)).astype(bf16).T,
            jnp.concatenate(dv, 0).astype(bf16).T,
        ],
        1,
    )
    yield
    gq[...] += dot(y, dqkv, 0, 0)
    d_shift = dot(dqkv, w_qkv[...], 1, 1).astype(bf16).astype(f32)
    result[at] = dx1 + layer_norm_backward(d_shift, g1, xhat1, rstd1)
    yield


def take_turns(stages):
    while stages:
        stages = [one for one in stages if next(one, stages) is not stages]


def halves(tile):
    return tile.reshape(tile.shape[0] // 2, 2 * tile.shape[1], tile.shape[2]).astype(bf16)


def unhalves(packed):
    return packed.astype(f32).reshape(packed.shape[0] * 2, packed.shape[1] // 2, packed.shape[2])


def block_kernel(
    n_row, n_col,
    frames_in, cotangent_in, gain1, w_qkv, bias_in, w_proj, gain2, w_up, w_down,
    grad, full_out,
    frames, cotangent, rel_bias,
    to_left, to_up, to_diag, from_right, from_down, from_diag,
    to_right, to_down, to_diag2, from_left, from_up, from_diag2,
    own_out, tile, probs, bias, gq, gp, gu, gd,
    red, red_send, red_core, red_x, red_z, red_y, full,
    load_sem, in_send, in_recv, out_send, out_recv, grad_sem, red_ssem, red_rsem,
):
    nfr, tile_h, tile_w, chan = frames.shape
    steps = nfr // PER
    row, col = lax.axis_index("row"), lax.axis_index("col")

    def loads(s):
        span = pl.ds(s * PER, PER)
        return [
            pltpu.make_async_copy(frames_in.at[span], frames.at[span], load_sem.at[0, s]),
            pltpu.make_async_copy(cotangent_in.at[span], cotangent.at[span], load_sem.at[1, s]),
        ]

    bias_load = pltpu.make_async_copy(bias_in, rel_bias, load_sem.at[0, steps])
    for s in range(min(2, steps)):
        for copy in loads(s):
            copy.start()
    bias_load.start()
    for s in range(2, steps):
        for copy in loads(s):
            copy.start()

    n_z = min(4, n_row)
    n_yh = n_row // n_z
    n_x = min(4, n_col // 2)
    n_yl = n_col // (2 * n_x)
    n_y = n_yh * n_yl
    core, x_at, y_lo = lax.rem(col, 2), lax.rem(col // 2, n_x), col // (2 * n_x)
    z_at, y_hi = lax.rem(row, n_z), row // n_z
    y_at = y_hi * n_yl + y_lo

    left, right = lax.rem(col + n_col - 1, n_col), lax.rem(col + 1, n_col)
    up, down = lax.rem(row + n_row - 1, n_row), lax.rem(row + 1, n_row)
    in_to = ((row, left), (up, col), (up, left))
    out_to = ((row, right), (down, col), (down, right))

    def core_peer(s):
        return (row, col + 1 - 2 * core)

    def x_peer(s):
        return (row, (y_lo * n_x + lax.rem(x_at + s, n_x)) * 2 + core)

    def z_peer(s):
        return (y_hi * n_z + lax.rem(z_at + s, n_z), col)

    def y_peer(s):
        other = lax.rem(y_at + s, n_y)
        return ((other // n_yl) * n_z + z_at, (lax.rem(other, n_yl) * n_x + x_at) * 2 + core)

    peers = list(in_to) + list(out_to) + [core_peer(1)]
    peers += [x_peer(s) for s in range(1, n_x)]
    peers += [z_peer(s) for s in range(1, n_z)]
    peers += [y_peer(s) for s in range(1, n_y)]
    barrier = pltpu.get_barrier_semaphore()
    for peer in peers:
        pl.semaphore_signal(barrier, inc=1, device_id=peer, device_id_type=MESH)
    pl.semaphore_wait(barrier, len(peers))

    def in_copies(s):
        span = pl.ds(s * PER, PER)
        pairs = ((to_left, from_right), (to_up, from_down), (to_diag, from_diag))
        return [
            pltpu.make_async_remote_copy(
                src_ref=a.at[span], dst_ref=b.at[span],
                send_sem=in_send.at[i, s], recv_sem=in_recv.at[i, s],
                device_id=in_to[i], device_id_type=MESH,
            )
            for i, (a, b) in enumerate(pairs)
        ]

    def out_copies(s):
        span = pl.ds(s * PER, PER)
        pairs = ((to_right, from_left), (to_down, from_up), (to_diag2, from_diag2))
        return [
            pltpu.make_async_remote_copy(
                src_ref=a.at[span], dst_ref=b.at[span],
                send_sem=out_send.at[i, s], recv_sem=out_recv.at[i, s],
                device_id=out_to[i], device_id_type=MESH,
            )
            for i, (a, b) in enumerate(pairs)
        ]

    def send_in(s):
        for copy in loads(s):
            copy.wait()
        for f in range(PER):
            at = s * PER + f
            for i, source in enumerate((frames, cotangent)):
                whole = source[at].astype(f32)
                to_left[at, i] = halves(whole[SHIFT:, :SHIFT])
                to_up[at, i] = halves(whole[:SHIFT, SHIFT:])
                to_diag[at, i] = halves(whole[:SHIFT, :SHIFT])
        for copy in in_copies(s):
            copy.start()

    def grad_copy(s):
        span = pl.ds(s * PER, PER)
        return pltpu.make_async_copy(tile.at[span], grad.at[span], grad_sem.at[s])

    def finish(s):
        for copy in out_copies(s):
            copy.wait_recv()
        for f in range(PER):
            at = s * PER + f
            top = jnp.concatenate([unhalves(from_diag2[at]), unhalves(from_up[at])], 1)
            tile[at, :SHIFT] = top.astype(bf16)
            rest = jnp.concatenate([unhalves(from_left[at]), unhalves(own_out[at])], 1)
            tile[at, SHIFT:] = rest.astype(bf16)
        grad_copy(s).start()

    ahead = min(2, steps)
    for s in range(ahead):
        send_in(s)

    bias_load.wait()
    wide = WS * WS
    at_q = lax.broadcasted_iota(jnp.int32, (wide, wide), 0)
    at_k = lax.broadcasted_iota(jnp.int32, (wide, wide), 1)
    cut_row = (at_q // (WS * SHIFT)) != (at_k // (WS * SHIFT))
    cut_col = (lax.rem(at_q, WS) // SHIFT) != (lax.rem(at_k, WS) // SHIFT)
    last_row = jnp.where(row == n_row - 1, 1.0, 0.0)
    last_col = jnp.where(col == n_col - 1, 1.0, 0.0)
    by_row = jnp.where(cut_row, last_row, 0.0)
    by_col = jnp.where(cut_col, last_col, 0.0)
    windows = tile_h // WS
    for w in range(windows):
        cut = jnp.maximum(by_row, by_col) if w == windows - 1 else by_col
        for h in range(HEADS):
            bias[w, h] = (rel_bias[h] + cut * -100.0) * LOG2E
    for ref in (gq, gp, gu, gd):
        ref[...] = jnp.zeros_like(ref)

    def step(s, carry):
        @pl.when(s + ahead < steps)
        def _():
            send_in(s + ahead)

        for copy in in_copies(s):
            copy.wait_recv()
        stages, result = [], [None] * (PER * windows)
        for f in range(PER):
            at = s * PER + f
            parts = []
            for i, source in enumerate((frames, cotangent)):
                own = source[at].astype(f32)[SHIFT:, SHIFT:]
                first = jnp.concatenate([own, unhalves(from_down[at, i])], 0)
                second = jnp.concatenate(
                    [unhalves(from_right[at, i]), unhalves(from_diag[at, i])], 0
                )
                parts.append(jnp.concatenate([first, second], 1))
            for w in range(windows):
                x, c = (p[w * WS : (w + 1) * WS].reshape(wide, chan) for p in parts)
                stages.append(
                    window_block(
                        f * windows + w, x, c, bias.at[w], gain1[...], gain2[...],
                        w_qkv, w_proj, w_up, w_down, probs, (gq, gp, gu, gd), result,
                    )
                )
        take_turns(stages)
        keep = tile_h - SHIFT
        for f in range(PER):
            at = s * PER + f
            out = [r.reshape(WS, WS, chan) for r in result[f * windows : (f + 1) * windows]]
            out = jnp.concatenate(out, 0)
            to_right[at] = halves(out[:keep, SHIFT:])
            to_down[at] = halves(out[keep:, :SHIFT])
            to_diag2[at] = halves(out[keep:, SHIFT:])
            own_out[at] = halves(out[:keep, :SHIFT])
        for copy in out_copies(s):
            copy.start()

        @pl.when(s >= 1)
        def _():
            finish(s - 1)

        return carry

    lax.fori_loop(0, steps, step, 0)

    for j in range(3):
        red[chan * j : chan * (j + 1)] = gq[:, chan * j : chan * (j + 1)]
    red[3 * chan : 4 * chan] = gp[...]
    for j in range(4):
        red[chan * (4 + j) : chan * (5 + j)] = gu[:, chan * j : chan * (j + 1)]
        red[chan * (8 + j) : chan * (9 + j)] = gd[:, chan * j : chan * (j + 1)]
    rows = red.shape[0]
    size_c = rows // 2
    size_x = size_c // n_x
    size_z = size_x // n_z

    def copy_to(peer, src, dst, sem):
        return pltpu.make_async_remote_copy(
            src_ref=src, dst_ref=dst, send_sem=red_ssem.at[sem], recv_sem=red_rsem.at[sem],
            device_id=peer, device_id_type=MESH,
        )

    def at(start, size):
        return pl.ds(pl.multiple_of(start, 16), size)

    red_send[...] = red[...].astype(bf16)
    sem = 0
    copies = []
    base = core * size_c
    first = copy_to(core_peer(1), red_send.at[at((1 - core) * size_c, size_c)], red_core, sem)
    first.start()
    copies.append(first)
    sem += 1
    finish(steps - 1)
    first.wait_recv()
    red[at(base, size_c)] += red_core[...].astype(f32)

    def reduce_stage(base, size, n, index, peer, landing, sem):
        red_send2 = red_stage[len(landings)]
        landings.append(0)
        red_send2[...] = red[at(base, size * n)].astype(bf16)
        started = []
        for s in range(1, n):
            other = lax.rem(index + s, n)
            started.append(
                copy_to(peer(s), red_send2.at[at(other * size, size)], landing.at[s - 1], sem)
            )
            started[-1].start()
            sem += 1
        base = base + index * size
        for copy in started:
            copy.wait_recv()
        total = red[at(base, size)]
        for s in range(1, n):
            total += landing[s - 1].astype(f32)
        red[at(base, size)] = total
        copies.extend(started)
        return base, sem

    landings = []
    red_stage = (full.at[pl.ds(rows, size_c)], full.at[pl.ds(rows + size_c, size_x)])
    base, sem = reduce_stage(base, size_x, n_x, x_at, x_peer, red_x, sem)
    base, sem = reduce_stage(base, size_z, n_z, z_at, z_peer, red_z, sem)
    red_y[y_at] = red[at(base, size_z)].astype(bf16)
    started = []
    for s in range(1, n_y):
        started.append(copy_to(y_peer(s), red_y.at[y_at], red_y.at[y_at], sem))
        started[-1].start()
        sem += 1
    for copy in started:
        copy.wait_recv()
    copies.extend(started)
    total = red_y[0].astype(f32)
    for j in range(1, n_y):
        total += red_y[j].astype(f32)
    full[at(base, size_z)] = total.astype(bf16)

    def gather_stage(base, size, n, peer, sem):
        started = []
        for s in range(1, n):
            part = full.at[at(base, size)]
            started.append(copy_to(peer(s), part, part, sem))
            started[-1].start()
            sem += 1
        for copy in started:
            copy.wait_recv()
        copies.extend(started)
        return sem

    sem = gather_stage(base, size_z, n_z, z_peer, sem)
    sem = gather_stage(core * size_c + x_at * size_x, size_x, n_x, x_peer, sem)
    sem = gather_stage(core * size_c, size_c, 2, core_peer, sem)
    full_out[...] = full[:rows]
    for copy in copies:
        copy.wait_send()

    def drain(s, carry):
        for copy in in_copies(s) + out_copies(s):
            copy.wait_send()
        grad_copy(s).wait()
        return carry

    lax.fori_loop(0, steps, drain, 0)


def finish_kernel(factor, grad_b, full, grad, g_qkv, g_proj, g_up, g_down):
    grad[...] = grad_b[...].astype(f32)

    @pl.when(pl.program_id(0) == 0)
    def _():
        chan = full.shape[1]

        def block(j):
            return full[chan * j : chan * (j + 1)].astype(f32) * factor

        for j in range(g_qkv.shape[1] // chan):
            g_qkv[:, chan * j : chan * (j + 1)] = block(j)
        g_proj[...] = block(3)
        for j in range(g_up.shape[1] // chan):
            g_up[:, chan * j : chan * (j + 1)] = block(4 + j)
            g_down[chan * j : chan * (j + 1)] = block(8 + j).T


def solution(mesh):
    n_row, n_col = mesh.shape["row"], mesh.shape["col"]

    def shards(frames, cotangent, gain1, w_qkv, rel_bias, w_proj, gain2, w_up, w_down):
        nfr, tile_h, tile_w, chan = frames.shape
        ff = w_up.shape[1]
        factor = float(nfr * tile_h * tile_w * n_row * n_col) ** -0.5
        long, short = (tile_h - SHIFT) // 2, SHIFT // 2
        wide = WS * WS
        rows = 4 * chan + 2 * ff
        n_z, n_x = min(4, n_row), min(4, n_col // 2)
        n_y = (n_row // n_z) * (n_col // (2 * n_x))
        size_c = rows // 2
        size_x = size_c // n_x
        size_z = size_x // n_z
        n_sem = 2 + 2 * (n_x - 1) + 2 * (n_z - 1) + (n_y - 1)

        def pieces(k):
            sizes = (long, short, short)
            lead = (nfr,) if k == 1 else (nfr, k)
            return [pltpu.VMEM(lead + (n, 2 * SHIFT, chan), bf16) for n in sizes]

        vmem = pl.BlockSpec(memory_space=pltpu.VMEM)
        hbm = pl.BlockSpec(memory_space=pl.ANY)
        steps, windows = nfr // PER, tile_h // WS
        grad_b, full = pl.pallas_call(
            functools.partial(block_kernel, n_row, n_col),
            out_shape=[
                jax.ShapeDtypeStruct(frames.shape, bf16),
                jax.ShapeDtypeStruct((rows, chan), bf16),
            ],
            in_specs=[hbm, hbm, vmem, vmem, hbm, vmem, vmem, vmem, vmem],
            out_specs=[hbm, vmem],
            scratch_shapes=[
                pltpu.VMEM(frames.shape, bf16),
                pltpu.VMEM(frames.shape, bf16),
                pltpu.VMEM(rel_bias.shape, f32),
            ]
            + pieces(2) + pieces(2) + pieces(1) + pieces(1)
            + [
                pltpu.VMEM((nfr, long, 2 * SHIFT, chan), bf16),
                pltpu.VMEM(frames.shape, bf16),
                pltpu.VMEM((PER * windows, HEADS, wide, wide), bf16),
                pltpu.VMEM((windows, HEADS, wide, wide), f32),
                pltpu.VMEM((chan, 3 * chan), f32),
                pltpu.VMEM((chan, chan), f32),
                pltpu.VMEM((chan, ff), f32),
                pltpu.VMEM((chan, ff), f32),
                pltpu.VMEM((rows, chan), f32),
                pltpu.VMEM((rows, chan), bf16),
                pltpu.VMEM((size_c, chan), bf16),
                pltpu.VMEM((max(n_x - 1, 1), size_x, chan), bf16),
                pltpu.VMEM((max(n_z - 1, 1), size_z, chan), bf16),
                pltpu.VMEM((n_y, size_z, chan), bf16),
                pltpu.VMEM((rows + size_c + size_x, chan), bf16),
                pltpu.SemaphoreType.DMA((2, steps + 1)),
                pltpu.SemaphoreType.DMA((3, steps)),
                pltpu.SemaphoreType.DMA((3, steps)),
                pltpu.SemaphoreType.DMA((3, steps)),
                pltpu.SemaphoreType.DMA((3, steps)),
                pltpu.SemaphoreType.DMA((steps,)),
                pltpu.SemaphoreType.DMA((n_sem,)),
                pltpu.SemaphoreType.DMA((n_sem,)),
            ],
            compiler_params=pltpu.CompilerParams(
                collective_id=0, has_side_effects=True, vmem_limit_bytes=56 * 2**20
            ),
        )(
            frames, cotangent, gain1.reshape(1, chan), w_qkv, rel_bias, w_proj,
            gain2.reshape(1, chan), w_up, w_down,
        )

        def whole(shape):
            return pl.BlockSpec(shape, lambda i: (0, 0))

        chunk = pl.BlockSpec((PER,) + frames.shape[1:], lambda i: (i, 0, 0, 0))
        sizes = [(chan, 3 * chan), (chan, chan), (chan, ff), (ff, chan)]
        return pl.pallas_call(
            functools.partial(finish_kernel, factor),
            grid=(steps,),
            out_shape=[jax.ShapeDtypeStruct(frames.shape, f32)]
            + [jax.ShapeDtypeStruct(size, f32) for size in sizes],
            in_specs=[chunk, whole((rows, chan))],
            out_specs=[chunk] + [whole(size) for size in sizes],
            compiler_params=pltpu.CompilerParams(vmem_limit_bytes=32 * 2**20),
        )(grad_b, full)

    tiles = P(None, "row", "col", None)
    return jax.shard_map(
        shards,
        mesh=mesh,
        in_specs=(tiles, tiles) + (P(),) * 7,
        out_specs=(tiles, P(), P(), P(), P()),
        check_vma=False,
    )
```

```python
import functools
import math

import jax
import jax.numpy as jnp
from jax import lax
from jax.experimental import pallas as pl
from jax.experimental.pallas import tpu as pltpu
from jax.sharding import PartitionSpec as P

HEADS = 4
WS = 16
SHIFT = 8
EPS = 1e-05
LOG2E = math.log2(math.e)
MESH = pl.DeviceIdType.MESH
bf16 = jnp.bfloat16
f32 = jnp.float32
PER = 2


def dot(a, b, ca, cb):
    return lax.dot_general(a, b, (((ca,), (cb,)), ((), ())), preferred_element_type=f32)


def layer_norm_stats(x):
    centered = x - jnp.mean(x, -1, keepdims=True)
    rstd = lax.rsqrt(jnp.mean(centered * centered, -1, keepdims=True) + EPS)
    return centered * rstd, rstd


def layer_norm_backward(dy, gain, xhat, rstd):
    dxh = dy * gain
    return rstd * (
        dxh
        - jnp.mean(dxh, -1, keepdims=True)
        - xhat * jnp.mean(dxh * xhat, -1, keepdims=True)
    )


def gelu_and_slope(u):
    expo = jnp.exp2(u * u * (-0.5 * LOG2E))
    t = 1.0 / (1.0 + (0.3275911 / math.sqrt(2.0)) * jnp.abs(u))
    poly = 0.5 * 1.061405429
    for c in (-1.453152027, 1.421413741, -0.284496736, 0.254829592):
        poly = t * poly + 0.5 * c
    tail = t * poly * expo
    cdf = jnp.where(u < 0.0, tail, 1.0 - tail)
    return u * cdf, cdf + u * expo * (1.0 / math.sqrt(2.0 * math.pi))


def window_block(at, x, c, bias, g1, g2, w_qkv, w_proj, w_up, w_down, probs, acc, result):
    gq, gp, gu, gd = acc
    tokens, chan = x.shape
    hd = chan // HEADS
    ff = w_up.shape[1]
    head = lax.broadcasted_iota(jnp.int32, (tokens, chan), 1) // hd
    xhat1, rstd1 = layer_norm_stats(x)
    y = (xhat1 * g1).astype(bf16)
    yield
    qkv = dot(y, w_qkv[...], 1, 0)
    yield
    q = qkv[:, :chan] * (LOG2E / math.sqrt(hd))
    k = qkv[:, chan : 2 * chan].astype(bf16)
    v_one = jnp.concatenate([qkv[:, 2 * chan :].astype(bf16), jnp.ones((tokens, chan), bf16)], 1)
    yield
    total, norm = None, None
    for h in range(HEADS):
        mine = head == h
        scores = dot(jnp.where(mine, q, 0.0).astype(bf16), k, 1, 1) + bias[h]
        yield
        expo = jnp.exp2(scores - jnp.max(scores, -1, keepdims=True)).astype(bf16)
        probs[at, h] = expo
        yield
        out = dot(expo, v_one, 1, 0)
        total = out[:, :chan] if h == 0 else jnp.where(mine, out[:, :chan], total)
        norm = out[:, chan:] if h == 0 else jnp.where(mine, out[:, chan:], norm)
        yield
    inverse = 1.0 / norm
    attended = total * inverse
    attended_b = attended.astype(bf16)
    proj = dot(attended_b, w_proj[...], 1, 0).astype(bf16)
    yield
    x1 = (x + proj.astype(f32)).astype(bf16).astype(f32)
    xhat2, rstd2 = layer_norm_stats(x1)
    z = (xhat2 * g2).astype(bf16)
    c_b = c.astype(bf16)
    yield
    z_t, c_t = z.T, c_b.T
    dz = None
    part = ff // 2
    for j in range(0, ff, part):
        u = dot(z, w_up[:, j : j + part], 1, 0)
        d_hid = dot(c_b, w_down[j : j + part, :], 1, 1)
        yield
        act, slope = gelu_and_slope(u)
        hid = act.astype(bf16)
        du = (d_hid * slope).astype(bf16)
        yield
        gd[:, j : j + part] += dot(c_t, hid, 1, 0)
        gu[:, j : j + part] += dot(z_t, du, 1, 0)
        more = dot(du, w_up[:, j : j + part], 1, 1)
        dz = more if dz is None else dz + more
        yield
    dx1 = c + layer_norm_backward(dz, g2, xhat2, rstd2)
    dx1_b = dx1.astype(bf16)
    gp[...] += dot(attended_b, dx1_b, 0, 0)
    d_att = dot(dx1_b, w_proj[...], 1, 1).astype(bf16).astype(f32)
    yield
    d_att = d_att * inverse
    d_sum = -(d_att * attended)
    q_t = q.astype(bf16).T
    d_att_t = d_att.astype(bf16).T
    yield
    dv, dk, dq = [], [], None
    for h in range(HEADS):
        mine = head == h
        left = jnp.concatenate(
            [jnp.where(mine, d_att, 0.0).astype(bf16), jnp.where(mine, d_sum, 0.0).astype(bf16)], 1
        )
        d_prob = dot(left, v_one, 1, 1)
        yield
        expo = probs[at, h]
        ds = (expo.astype(f32) * d_prob).astype(bf16)
        yield
        dv.append(dot(d_att_t[hd * h : hd * (h + 1)], expo, 1, 0))
        dk.append(dot(q_t[hd * h : hd * (h + 1)], ds, 1, 0))
        out = dot(ds, k, 1, 0)
        dq = out if h == 0 else jnp.where(mine, out, dq)
        yield
    dqkv = jnp.concatenate(
        [
            (dq * hd**-0.5).astype(bf16),
            (jnp.concatenate(dk, 0) * (1.0 / LOG2E)).astype(bf16).T,
            jnp.concatenate(dv, 0).astype(bf16).T,
        ],
        1,
    )
    yield
    gq[...] += dot(y, dqkv, 0, 0)
    d_shift = dot(dqkv, w_qkv[...], 1, 1).astype(bf16).astype(f32)
    result[at] = dx1 + layer_norm_backward(d_shift, g1, xhat1, rstd1)
    yield


def take_turns(stages):
    while stages:
        stages = [one for one in stages if next(one, stages) is not stages]


def halves(tile):
    return tile.reshape(tile.shape[0] // 2, 2 * tile.shape[1], tile.shape[2]).astype(bf16)


def unhalves(packed):
    return packed.astype(f32).reshape(packed.shape[0] * 2, packed.shape[1] // 2, packed.shape[2])


def block_kernel(
    n_row, n_col,
    frames_in, cotangent_in, gain1, w_qkv, bias_in, w_proj, gain2, w_up, w_down,
    grad, full_out,
    frames, cotangent, rel_bias,
    to_side, to_row, to_corner, from_side, from_row, from_corner,
    back_side, back_row, back_corner, got_side, got_row, got_corner,
    own_out, tile, probs, bias, gq, gp, gu, gd,
    red, red_send, red_core, red_plane, red_y, full,
    load_sem, in_send, in_recv, out_send, out_recv, grad_sem, red_ssem, red_rsem,
):
    nfr, tile_h, tile_w, chan = frames.shape
    steps = nfr // PER
    row, col = lax.axis_index("row"), lax.axis_index("col")

    def loads(s):
        span = pl.ds(s * PER, PER)
        return [
            pltpu.make_async_copy(frames_in.at[span], frames.at[span], load_sem.at[0, s]),
            pltpu.make_async_copy(cotangent_in.at[span], cotangent.at[span], load_sem.at[1, s]),
        ]

    bias_load = pltpu.make_async_copy(bias_in, rel_bias, load_sem.at[0, steps])
    for s in range(min(2, steps)):
        for copy in loads(s):
            copy.start()
    bias_load.start()
    for s in range(2, steps):
        for copy in loads(s):
            copy.start()

    n_z = min(4, n_row)
    n_yh = n_row // n_z
    n_x = min(4, n_col // 2)
    n_yl = n_col // (2 * n_x)
    n_y = n_yh * n_yl
    core, x_at, y_lo = lax.rem(col, 2), lax.rem(col // 2, n_x), col // (2 * n_x)
    z_at, y_hi = lax.rem(row, n_z), row // n_z
    y_at = y_hi * n_yl + y_lo

    left, right = lax.rem(col + n_col - 1, n_col), lax.rem(col + 1, n_col)
    up, down = lax.rem(row + n_row - 1, n_row), lax.rem(row + 1, n_row)
    ways = (((row, left), (up, col), (up, left)), ((row, right), (down, col), (down, right)))

    def core_peer(s):
        return (row, col + 1 - 2 * core)

    plane_at = z_at * n_x + x_at

    def plane_peer(s):
        other = lax.rem(plane_at + s, n_x * n_z)
        return (y_hi * n_z + other // n_x, (y_lo * n_x + lax.rem(other, n_x)) * 2 + core)

    def y_peer(s):
        other = lax.rem(y_at + s, n_y)
        return ((other // n_yl) * n_z + z_at, (lax.rem(other, n_yl) * n_x + x_at) * 2 + core)

    peers = list(ways[0]) + list(ways[1]) + [core_peer(1)]
    peers += [plane_peer(s) for s in range(1, n_x * n_z)]
    peers += [y_peer(s) for s in range(1, n_y)]
    barrier = pltpu.get_barrier_semaphore()
    for peer in peers:
        pl.semaphore_signal(barrier, inc=1, device_id=peer, device_id_type=MESH)
    pl.semaphore_wait(barrier, len(peers))

    def in_copies(s):
        pairs = ((to_side, from_side), (to_row, from_row), (to_corner, from_corner))
        return [
            pltpu.make_async_remote_copy(
                src_ref=a.at[s * PER + f], dst_ref=b.at[s * PER + f],
                send_sem=in_send.at[i, s * PER + f], recv_sem=in_recv.at[i, s * PER + f],
                device_id=ways[f][i], device_id_type=MESH,
            )
            for f in range(PER)
            for i, (a, b) in enumerate(pairs)
        ]

    def out_copies(s):
        pairs = ((back_side, got_side), (back_row, got_row), (back_corner, got_corner))
        return [
            pltpu.make_async_remote_copy(
                src_ref=a.at[s * PER + f], dst_ref=b.at[s * PER + f],
                send_sem=out_send.at[i, s * PER + f], recv_sem=out_recv.at[i, s * PER + f],
                device_id=ways[1 - f][i], device_id_type=MESH,
            )
            for f in range(PER)
            for i, (a, b) in enumerate(pairs)
        ]

    def send_in(s):
        for copy in loads(s):
            copy.wait()
        for f in range(PER):
            at = s * PER + f
            rows_near, rows_far, cols_near, cols_far = cuts[f]
            for i, source in enumerate((frames, cotangent)):
                whole = source[at].astype(f32)
                to_side[at, i] = halves(whole[rows_near, cols_far])
                to_row[at, i] = halves(whole[rows_far, cols_near])
                to_corner[at, i] = halves(whole[rows_far, cols_far])
        for copy in in_copies(s):
            copy.start()

    keep = tile_h - SHIFT
    cuts = (
        (slice(SHIFT, None), slice(0, SHIFT), slice(SHIFT, None), slice(0, SHIFT)),
        (slice(0, keep), slice(keep, None), slice(0, SHIFT), slice(SHIFT, None)),
    )

    def put(f, kept, side, over, corner):
        order = (lambda a, b: (a, b)) if f == 0 else (lambda a, b: (b, a))
        body = jnp.concatenate(order(kept, side), 1)
        edge = jnp.concatenate(order(over, corner), 1)
        return jnp.concatenate(order(body, edge), 0)

    def grad_copy(s):
        span = pl.ds(s * PER, PER)
        return pltpu.make_async_copy(tile.at[span], grad.at[span], grad_sem.at[s])

    def finish(s):
        for copy in out_copies(s):
            copy.wait_recv()
        for f in range(PER):
            at = s * PER + f
            parts = (own_out, got_side, got_row, got_corner)
            tile[at] = put(1 - f, *(unhalves(p[at]) for p in parts)).astype(bf16)
        grad_copy(s).start()

    send_in(0)

    bias_load.wait()
    wide = WS * WS
    at_q = lax.broadcasted_iota(jnp.int32, (wide, wide), 0)
    at_k = lax.broadcasted_iota(jnp.int32, (wide, wide), 1)
    cut_row = (at_q // (WS * SHIFT)) != (at_k // (WS * SHIFT))
    cut_col = (lax.rem(at_q, WS) // SHIFT) != (lax.rem(at_k, WS) // SHIFT)
    windows = tile_h // WS
    for f in range(PER):
        last_row = jnp.where(row == (n_row - 1 if f == 0 else 0), 1.0, 0.0)
        last_col = jnp.where(col == (n_col - 1 if f == 0 else 0), 1.0, 0.0)
        by_row = jnp.where(cut_row, last_row, 0.0)
        by_col = jnp.where(cut_col, last_col, 0.0)
        for w in range(windows):
            at_edge = w == (windows - 1 if f == 0 else 0)
            cut = jnp.maximum(by_row, by_col) if at_edge else by_col
            for h in range(HEADS):
                bias[f, w, h] = (rel_bias[h] + cut * -100.0) * LOG2E
    for ref in (gq, gp, gu, gd):
        ref[...] = jnp.zeros_like(ref)

    def arrive(s):
        for copy in in_copies(s):
            copy.wait_recv()

    arrive(0)
    if steps > 1:
        send_in(1)

    def step(s, carry):
        @pl.when(s + 2 < steps)
        def _():
            send_in(s + 2)

        stages, result = [], [None] * (PER * windows)
        for f in range(PER):
            at = s * PER + f
            parts = []
            for i, source in enumerate((frames, cotangent)):
                own = source[at].astype(f32)[cuts[f][0], cuts[f][2]]
                got = (unhalves(p[at, i]) for p in (from_side, from_row, from_corner))
                parts.append(put(f, own, *got))
            for w in range(windows):
                x, c = (p[w * WS : (w + 1) * WS].reshape(wide, chan) for p in parts)
                stages.append(
                    window_block(
                        f * windows + w, x, c, bias.at[f, w], gain1[...], gain2[...],
                        w_qkv, w_proj, w_up, w_down, probs, (gq, gp, gu, gd), result,
                    )
                )
        take_turns(stages)
        for f in range(PER):
            at = s * PER + f
            out = [r.reshape(WS, WS, chan) for r in result[f * windows : (f + 1) * windows]]
            out = jnp.concatenate(out, 0)
            if f == 0:
                rows_own, rows_far = slice(0, keep), slice(keep, None)
                cols_own, cols_far = slice(0, SHIFT), slice(SHIFT, None)
            else:
                rows_own, rows_far = slice(SHIFT, None), slice(0, SHIFT)
                cols_own, cols_far = slice(SHIFT, None), slice(0, SHIFT)
            back_side[at] = halves(out[rows_own, cols_far])
            back_row[at] = halves(out[rows_far, cols_own])
            back_corner[at] = halves(out[rows_far, cols_far])
            own_out[at] = halves(out[rows_own, cols_own])
        for copy in out_copies(s):
            copy.start()

        @pl.when(s >= 1)
        def _():
            finish(s - 1)

        @pl.when(s + 1 < steps)
        def _():
            arrive(s + 1)

        return carry

    lax.fori_loop(0, steps, step, 0)

    for j in range(3):
        red[chan * j : chan * (j + 1)] = gq[:, chan * j : chan * (j + 1)]
    red[3 * chan : 4 * chan] = gp[...]
    for j in range(4):
        red[chan * (4 + j) : chan * (5 + j)] = gu[:, chan * j : chan * (j + 1)]
        red[chan * (8 + j) : chan * (9 + j)] = gd[:, chan * j : chan * (j + 1)]
    rows = red.shape[0]
    size_c = rows // 2
    size_z = size_c // (n_x * n_z)

    def copy_to(peer, src, dst, sem):
        return pltpu.make_async_remote_copy(
            src_ref=src, dst_ref=dst, send_sem=red_ssem.at[sem], recv_sem=red_rsem.at[sem],
            device_id=peer, device_id_type=MESH,
        )

    def at(start, size):
        return pl.ds(pl.multiple_of(start, 16), size)

    red_send[...] = red[...].astype(bf16)
    sem = 0
    copies = []
    base = core * size_c
    first = copy_to(core_peer(1), red_send.at[at((1 - core) * size_c, size_c)], red_core, sem)
    first.start()
    copies.append(first)
    sem += 1
    finish(steps - 1)
    first.wait_recv()
    red[at(base, size_c)] += red_core[...].astype(f32)

    def reduce_stage(base, size, n, index, peer, landing, sem):
        red_send2 = red_stage[len(landings)]
        landings.append(0)
        red_send2[...] = red[at(base, size * n)].astype(bf16)
        started = []
        for s in range(1, n):
            other = lax.rem(index + s, n)
            started.append(
                copy_to(peer(s), red_send2.at[at(other * size, size)], landing.at[s - 1], sem)
            )
            started[-1].start()
            sem += 1
        base = base + index * size
        for copy in started:
            copy.wait_recv()
        total = red[at(base, size)]
        for s in range(1, n):
            total += landing[s - 1].astype(f32)
        red[at(base, size)] = total
        copies.extend(started)
        return base, sem

    landings = []
    red_stage = (full.at[pl.ds(rows, size_c)],)
    base, sem = reduce_stage(base, size_z, n_x * n_z, plane_at, plane_peer, red_plane, sem)
    red_y[y_at] = red[at(base, size_z)].astype(bf16)
    started = []
    for s in range(1, n_y):
        started.append(copy_to(y_peer(s), red_y.at[y_at], red_y.at[y_at], sem))
        started[-1].start()
        sem += 1
    for copy in started:
        copy.wait_recv()
    copies.extend(started)
    total = red_y[0].astype(f32)
    for j in range(1, n_y):
        total += red_y[j].astype(f32)
    full[at(base, size_z)] = total.astype(bf16)

    def gather_stage(base, size, n, peer, sem):
        started = []
        for s in range(1, n):
            part = full.at[at(base, size)]
            started.append(copy_to(peer(s), part, part, sem))
            started[-1].start()
            sem += 1
        for copy in started:
            copy.wait_recv()
        copies.extend(started)
        return sem

    sem = gather_stage(base, size_z, n_x * n_z, plane_peer, sem)
    sem = gather_stage(core * size_c, size_c, 2, core_peer, sem)
    full_out[...] = full[:rows]
    for copy in copies:
        copy.wait_send()

    def drain(s, carry):
        for copy in in_copies(s) + out_copies(s):
            copy.wait_send()
        grad_copy(s).wait()
        return carry

    lax.fori_loop(0, steps, drain, 0)


def finish_kernel(factor, grad_b, full, grad, g_qkv, g_proj, g_up, g_down):
    grad[...] = grad_b[...].astype(f32)

    @pl.when(pl.program_id(0) == 0)
    def _():
        chan = full.shape[1]

        def block(j):
            return full[chan * j : chan * (j + 1)].astype(f32) * factor

        for j in range(g_qkv.shape[1] // chan):
            g_qkv[:, chan * j : chan * (j + 1)] = block(j)
        g_proj[...] = block(3)
        for j in range(g_up.shape[1] // chan):
            g_up[:, chan * j : chan * (j + 1)] = block(4 + j)
            g_down[chan * j : chan * (j + 1)] = block(8 + j).T


def solution(mesh):
    n_row, n_col = mesh.shape["row"], mesh.shape["col"]

    def shards(frames, cotangent, gain1, w_qkv, rel_bias, w_proj, gain2, w_up, w_down):
        nfr, tile_h, tile_w, chan = frames.shape
        ff = w_up.shape[1]
        factor = float(nfr * tile_h * tile_w * n_row * n_col) ** -0.5
        long, short = (tile_h - SHIFT) // 2, SHIFT // 2
        wide = WS * WS
        rows = 4 * chan + 2 * ff
        n_z, n_x = min(4, n_row), min(4, n_col // 2)
        n_y = (n_row // n_z) * (n_col // (2 * n_x))
        size_c = rows // 2
        size_z = size_c // (n_x * n_z)
        n_sem = 2 + 2 * (n_x * n_z - 1) + (n_y - 1)

        def pieces(k):
            sizes = (long, short, short)
            lead = (nfr,) if k == 1 else (nfr, k)
            return [pltpu.VMEM(lead + (n, 2 * SHIFT, chan), bf16) for n in sizes]

        vmem = pl.BlockSpec(memory_space=pltpu.VMEM)
        hbm = pl.BlockSpec(memory_space=pl.ANY)
        steps, windows = nfr // PER, tile_h // WS
        grad_b, full = pl.pallas_call(
            functools.partial(block_kernel, n_row, n_col),
            out_shape=[
                jax.ShapeDtypeStruct(frames.shape, bf16),
                jax.ShapeDtypeStruct((rows, chan), bf16),
            ],
            in_specs=[hbm, hbm, vmem, vmem, hbm, vmem, vmem, vmem, vmem],
            out_specs=[hbm, vmem],
            scratch_shapes=[
                pltpu.VMEM(frames.shape, bf16),
                pltpu.VMEM(frames.shape, bf16),
                pltpu.VMEM(rel_bias.shape, f32),
            ]
            + pieces(2) + pieces(2) + pieces(1) + pieces(1)
            + [
                pltpu.VMEM((nfr, long, 2 * SHIFT, chan), bf16),
                pltpu.VMEM(frames.shape, bf16),
                pltpu.VMEM((PER * windows, HEADS, wide, wide), bf16),
                pltpu.VMEM((PER, windows, HEADS, wide, wide), f32),
                pltpu.VMEM((chan, 3 * chan), f32),
                pltpu.VMEM((chan, chan), f32),
                pltpu.VMEM((chan, ff), f32),
                pltpu.VMEM((chan, ff), f32),
                pltpu.VMEM((rows, chan), f32),
                pltpu.VMEM((rows, chan), bf16),
                pltpu.VMEM((size_c, chan), bf16),
                pltpu.VMEM((n_x * n_z - 1, size_z, chan), bf16),
                pltpu.VMEM((n_y, size_z, chan), bf16),
                pltpu.VMEM((rows + size_c, chan), bf16),
                pltpu.SemaphoreType.DMA((2, steps + 1)),
                pltpu.SemaphoreType.DMA((3, nfr)),
                pltpu.SemaphoreType.DMA((3, nfr)),
                pltpu.SemaphoreType.DMA((3, nfr)),
                pltpu.SemaphoreType.DMA((3, nfr)),
                pltpu.SemaphoreType.DMA((steps,)),
                pltpu.SemaphoreType.DMA((n_sem,)),
                pltpu.SemaphoreType.DMA((n_sem,)),
            ],
            compiler_params=pltpu.CompilerParams(
                collective_id=0, has_side_effects=True, vmem_limit_bytes=56 * 2**20
            ),
        )(
            frames, cotangent, gain1.reshape(1, chan), w_qkv, rel_bias, w_proj,
            gain2.reshape(1, chan), w_up, w_down,
        )

        def whole(shape):
            return pl.BlockSpec(shape, lambda i: (0, 0))

        chunk = pl.BlockSpec((PER,) + frames.shape[1:], lambda i: (i, 0, 0, 0))
        sizes = [(chan, 3 * chan), (chan, chan), (chan, ff), (ff, chan)]
        return pl.pallas_call(
            functools.partial(finish_kernel, factor),
            grid=(steps,),
            out_shape=[jax.ShapeDtypeStruct(frames.shape, f32)]
            + [jax.ShapeDtypeStruct(size, f32) for size in sizes],
            in_specs=[chunk, whole((rows, chan))],
            out_specs=[chunk] + [whole(size) for size in sizes],
            compiler_params=pltpu.CompilerParams(vmem_limit_bytes=60 * 2**20),
        )(grad_b, full)

    tiles = P(None, "row", "col", None)
    return jax.shard_map(
        shards,
        mesh=mesh,
        in_specs=(tiles, tiles) + (P(),) * 7,
        out_specs=(tiles, P(), P(), P(), P()),
        check_vma=False,
    )
```

```python
import functools
import math

import jax
import jax.numpy as jnp
from jax import lax
from jax.experimental import pallas as pl
from jax.experimental.pallas import tpu as pltpu
from jax.sharding import PartitionSpec as P

HEADS = 4
WS = 16
SHIFT = 8
EPS = 1e-05
LOG2E = math.log2(math.e)
MESH = pl.DeviceIdType.MESH
bf16 = jnp.bfloat16
f32 = jnp.float32
PER = 2


def dot(a, b, ca, cb):
    return lax.dot_general(a, b, (((ca,), (cb,)), ((), ())), preferred_element_type=f32)


def layer_norm_stats(x):
    centered = x - jnp.mean(x, -1, keepdims=True)
    rstd = lax.rsqrt(jnp.mean(centered * centered, -1, keepdims=True) + EPS)
    return centered * rstd, rstd


def layer_norm_backward(dy, gain, xhat, rstd):
    dxh = dy * gain
    return rstd * (
        dxh
        - jnp.mean(dxh, -1, keepdims=True)
        - xhat * jnp.mean(dxh * xhat, -1, keepdims=True)
    )


def gelu_and_slope(u):
    expo = jnp.exp2(u * u * (-0.5 * LOG2E))
    p = math.sqrt(2.0) / 0.3275911
    t = 1.0 / (jnp.abs(u) + p)
    poly = 0.5 * 1.061405429 * p**5
    for n, c in ((4, -1.453152027), (3, 1.421413741), (2, -0.284496736), (1, 0.254829592)):
        poly = t * poly + 0.5 * c * p**n
    tail = t * poly * expo
    cdf = jnp.where(u < 0.0, tail, 1.0 - tail)
    return u * cdf, cdf + u * expo * (1.0 / math.sqrt(2.0 * math.pi))


def window_block(at, x, c, bias, g1, g2, w_qkv, w_proj, w_up, w_down, probs, acc, result):
    gq, gp, gu, gd = acc
    tokens, chan = x.shape
    hd = chan // HEADS
    ff = w_up.shape[1]
    head = lax.broadcasted_iota(jnp.int32, (tokens, chan), 1) // hd
    xhat1, rstd1 = layer_norm_stats(x)
    y = (xhat1 * g1).astype(bf16)
    yield
    qkv = dot(y, w_qkv[...], 1, 0)
    yield
    q = qkv[:, :chan] * (LOG2E / math.sqrt(hd))
    k = qkv[:, chan : 2 * chan].astype(bf16)
    v_one = jnp.concatenate([qkv[:, 2 * chan :].astype(bf16), jnp.ones((tokens, chan), bf16)], 1)
    yield
    total, norm = None, None
    for h in range(HEADS):
        mine = head == h
        scores = dot(jnp.where(mine, q, 0.0).astype(bf16), k, 1, 1) + bias[h]
        yield
        expo = jnp.exp2(scores - jnp.max(scores, -1, keepdims=True)).astype(bf16)
        probs[at, h] = expo
        yield
        out = dot(expo, v_one, 1, 0)
        total = out[:, :chan] if h == 0 else jnp.where(mine, out[:, :chan], total)
        norm = out[:, chan:] if h == 0 else jnp.where(mine, out[:, chan:], norm)
        yield
    inverse = 1.0 / norm
    attended = total * inverse
    attended_b = attended.astype(bf16)
    proj = dot(attended_b, w_proj[...], 1, 0).astype(bf16)
    yield
    x1 = (x + proj.astype(f32)).astype(bf16).astype(f32)
    xhat2, rstd2 = layer_norm_stats(x1)
    z = (xhat2 * g2).astype(bf16)
    c_b = c.astype(bf16)
    yield
    z_t, c_t = z.T, c_b.T
    dz = None
    part = ff // 2
    for j in range(0, ff, part):
        u = dot(z, w_up[:, j : j + part], 1, 0)
        d_hid = dot(c_b, w_down[j : j + part, :], 1, 1)
        yield
        act, slope = gelu_and_slope(u)
        hid = act.astype(bf16)
        du = (d_hid * slope).astype(bf16)
        yield
        gd[:, j : j + part] += dot(c_t, hid, 1, 0)
        gu[:, j : j + part] += dot(z_t, du, 1, 0)
        more = dot(du, w_up[:, j : j + part], 1, 1)
        dz = more if dz is None else dz + more
        yield
    dx1 = c + layer_norm_backward(dz, g2, xhat2, rstd2)
    dx1_b = dx1.astype(bf16)
    gp[...] += dot(attended_b, dx1_b, 0, 0)
    d_att = dot(dx1_b, w_proj[...], 1, 1).astype(bf16).astype(f32)
    yield
    d_att = d_att * inverse
    d_sum = -(d_att * attended)
    q_t = q.astype(bf16).T
    d_att_t = d_att.astype(bf16).T
    yield
    dv, dk, dq = [], [], None
    for h in range(HEADS):
        mine = head == h
        left = jnp.concatenate(
            [jnp.where(mine, d_att, 0.0).astype(bf16), jnp.where(mine, d_sum, 0.0).astype(bf16)], 1
        )
        d_prob = dot(left, v_one, 1, 1)
        yield
        expo = probs[at, h]
        ds = (expo.astype(f32) * d_prob).astype(bf16)
        yield
        dv.append(dot(d_att_t[hd * h : hd * (h + 1)], expo, 1, 0))
        dk.append(dot(q_t[hd * h : hd * (h + 1)], ds, 1, 0))
        out = dot(ds, k, 1, 0)
        dq = out if h == 0 else jnp.where(mine, out, dq)
        yield
    dqkv = jnp.concatenate(
        [
            (dq * hd**-0.5).astype(bf16),
            (jnp.concatenate(dk, 0) * (1.0 / LOG2E)).astype(bf16).T,
            jnp.concatenate(dv, 0).astype(bf16).T,
        ],
        1,
    )
    yield
    gq[...] += dot(y, dqkv, 0, 0)
    d_shift = dot(dqkv, w_qkv[...], 1, 1).astype(bf16).astype(f32)
    result[at] = dx1 + layer_norm_backward(d_shift, g1, xhat1, rstd1)
    yield


def take_turns(stages):
    while stages:
        stages = [one for one in stages if next(one, stages) is not stages]


def halves(tile):
    return tile.reshape(tile.shape[0] // 2, 2 * tile.shape[1], tile.shape[2]).astype(bf16)


def unhalves(packed):
    return packed.astype(f32).reshape(packed.shape[0] * 2, packed.shape[1] // 2, packed.shape[2])


def block_kernel(
    n_row, n_col,
    frames_in, cotangent_in, gain1, w_qkv, bias_in, w_proj, gain2, w_up, w_down,
    grad, full_out,
    frames, cotangent, rel_bias,
    to_side, to_row, to_corner, from_side, from_row, from_corner,
    back_side, back_row, back_corner, got_side, got_row, got_corner,
    own_out, tile, probs, bias, gq, gp, gu, gd,
    red, red_send, red_core, red_plane, red_y, full,
    load_sem, in_send, in_recv, out_send, out_recv, grad_sem, red_ssem, red_rsem,
):
    nfr, tile_h, tile_w, chan = frames.shape
    steps = nfr // PER
    row, col = lax.axis_index("row"), lax.axis_index("col")

    def loads(s):
        span = pl.ds(s * PER, PER)
        return [
            pltpu.make_async_copy(frames_in.at[span], frames.at[span], load_sem.at[0, s]),
            pltpu.make_async_copy(cotangent_in.at[span], cotangent.at[span], load_sem.at[1, s]),
        ]

    bias_load = pltpu.make_async_copy(bias_in, rel_bias, load_sem.at[0, steps])
    for s in range(min(2, steps)):
        for copy in loads(s):
            copy.start()
    bias_load.start()
    for s in range(2, steps):
        for copy in loads(s):
            copy.start()

    n_z = min(4, n_row)
    n_yh = n_row // n_z
    n_x = min(4, n_col // 2)
    n_yl = n_col // (2 * n_x)
    n_y = n_yh * n_yl
    core, x_at, y_lo = lax.rem(col, 2), lax.rem(col // 2, n_x), col // (2 * n_x)
    z_at, y_hi = lax.rem(row, n_z), row // n_z
    y_at = y_hi * n_yl + y_lo

    left, right = lax.rem(col + n_col - 1, n_col), lax.rem(col + 1, n_col)
    up, down = lax.rem(row + n_row - 1, n_row), lax.rem(row + 1, n_row)
    ways = (((row, left), (up, col), (up, left)), ((row, right), (down, col), (down, right)))

    def core_peer(s):
        return (row, col + 1 - 2 * core)

    plane_at = z_at * n_x + x_at

    def plane_peer(s):
        other = lax.rem(plane_at + s, n_x * n_z)
        return (y_hi * n_z + other // n_x, (y_lo * n_x + lax.rem(other, n_x)) * 2 + core)

    def y_peer(s):
        other = lax.rem(y_at + s, n_y)
        return ((other // n_yl) * n_z + z_at, (lax.rem(other, n_yl) * n_x + x_at) * 2 + core)

    peers = list(ways[0]) + list(ways[1]) + [core_peer(1)]
    peers += [plane_peer(s) for s in range(1, n_x * n_z)]
    peers += [y_peer(s) for s in range(1, n_y)]
    barrier = pltpu.get_barrier_semaphore()
    for peer in peers:
        pl.semaphore_signal(barrier, inc=1, device_id=peer, device_id_type=MESH)

    def in_copies(s):
        pairs = ((to_side, from_side), (to_row, from_row), (to_corner, from_corner))
        return [
            pltpu.make_async_remote_copy(
                src_ref=a.at[s * PER + f], dst_ref=b.at[s * PER + f],
                send_sem=in_send.at[i, s * PER + f], recv_sem=in_recv.at[i, s * PER + f],
                device_id=ways[f][i], device_id_type=MESH,
            )
            for f in range(PER)
            for i, (a, b) in enumerate(pairs)
        ]

    def out_copies(s):
        pairs = ((back_side, got_side), (back_row, got_row), (back_corner, got_corner))
        return [
            pltpu.make_async_remote_copy(
                src_ref=a.at[s * PER + f], dst_ref=b.at[s * PER + f],
                send_sem=out_send.at[i, s * PER + f], recv_sem=out_recv.at[i, s * PER + f],
                device_id=ways[1 - f][i], device_id_type=MESH,
            )
            for f in range(PER)
            for i, (a, b) in enumerate(pairs)
        ]

    def pack_in(s):
        for copy in loads(s):
            copy.wait()
        for f in range(PER):
            at = s * PER + f
            rows_near, rows_far, cols_near, cols_far = cuts[f]
            for i, source in enumerate((frames, cotangent)):
                whole = source[at].astype(f32)
                to_side[at, i] = halves(whole[rows_near, cols_far])
                to_row[at, i] = halves(whole[rows_far, cols_near])
                to_corner[at, i] = halves(whole[rows_far, cols_far])

    def send_in(s):
        pack_in(s)
        for copy in in_copies(s):
            copy.start()

    keep = tile_h - SHIFT
    cuts = (
        (slice(SHIFT, None), slice(0, SHIFT), slice(SHIFT, None), slice(0, SHIFT)),
        (slice(0, keep), slice(keep, None), slice(0, SHIFT), slice(SHIFT, None)),
    )

    def put(f, kept, side, over, corner):
        order = (lambda a, b: (a, b)) if f == 0 else (lambda a, b: (b, a))
        body = jnp.concatenate(order(kept, side), 1)
        edge = jnp.concatenate(order(over, corner), 1)
        return jnp.concatenate(order(body, edge), 0)

    def grad_copy(s):
        span = pl.ds(s * PER, PER)
        return pltpu.make_async_copy(tile.at[span], grad.at[span], grad_sem.at[s])

    def finish(s):
        for copy in out_copies(s):
            copy.wait_recv()
        for f in range(PER):
            at = s * PER + f
            parts = (own_out, got_side, got_row, got_corner)
            tile[at] = put(1 - f, *(unhalves(p[at]) for p in parts)).astype(bf16)
        grad_copy(s).start()

    pack_in(0)
    pl.semaphore_wait(barrier, len(peers))
    for copy in in_copies(0):
        copy.start()

    bias_load.wait()
    wide = WS * WS
    at_q = lax.broadcasted_iota(jnp.int32, (wide, wide), 0)
    at_k = lax.broadcasted_iota(jnp.int32, (wide, wide), 1)
    cut_row = (at_q // (WS * SHIFT)) != (at_k // (WS * SHIFT))
    cut_col = (lax.rem(at_q, WS) // SHIFT) != (lax.rem(at_k, WS) // SHIFT)
    windows = tile_h // WS
    for f in range(PER):
        last_row = jnp.where(row == (n_row - 1 if f == 0 else 0), 1.0, 0.0)
        last_col = jnp.where(col == (n_col - 1 if f == 0 else 0), 1.0, 0.0)
        by_row = jnp.where(cut_row, last_row, 0.0)
        by_col = jnp.where(cut_col, last_col, 0.0)
        for w in range(windows):
            at_edge = w == (windows - 1 if f == 0 else 0)
            cut = jnp.maximum(by_row, by_col) if at_edge else by_col
            for h in range(HEADS):
                bias[f, w, h] = (rel_bias[h] + cut * -100.0) * LOG2E
    for ref in (gq, gp, gu, gd):
        ref[...] = jnp.zeros_like(ref)

    def arrive(s):
        for copy in in_copies(s):
            copy.wait_recv()

    if steps > 1:
        send_in(1)
    arrive(0)

    def step(s, carry):
        @pl.when(s + 2 < steps)
        def _():
            send_in(s + 2)

        stages, result = [], [None] * (PER * windows)
        for f in range(PER):
            at = s * PER + f
            parts = []
            for i, source in enumerate((frames, cotangent)):
                own = source[at].astype(f32)[cuts[f][0], cuts[f][2]]
                got = (unhalves(p[at, i]) for p in (from_side, from_row, from_corner))
                parts.append(put(f, own, *got))
            for w in range(windows):
                x, c = (p[w * WS : (w + 1) * WS].reshape(wide, chan) for p in parts)
                stages.append(
                    window_block(
                        f * windows + w, x, c, bias.at[f, w], gain1[...], gain2[...],
                        w_qkv, w_proj, w_up, w_down, probs, (gq, gp, gu, gd), result,
                    )
                )
        take_turns(stages)
        for f in range(PER):
            at = s * PER + f
            out = [r.reshape(WS, WS, chan) for r in result[f * windows : (f + 1) * windows]]
            out = jnp.concatenate(out, 0)
            if f == 0:
                rows_own, rows_far = slice(0, keep), slice(keep, None)
                cols_own, cols_far = slice(0, SHIFT), slice(SHIFT, None)
            else:
                rows_own, rows_far = slice(SHIFT, None), slice(0, SHIFT)
                cols_own, cols_far = slice(SHIFT, None), slice(0, SHIFT)
            back_side[at] = halves(out[rows_own, cols_far])
            back_row[at] = halves(out[rows_far, cols_own])
            back_corner[at] = halves(out[rows_far, cols_far])
            own_out[at] = halves(out[rows_own, cols_own])
        for copy in out_copies(s):
            copy.start()

        @pl.when(s >= 2)
        def _():
            finish(s - 2)

        @pl.when(s + 1 < steps)
        def _():
            arrive(s + 1)

        return carry

    lax.fori_loop(0, steps, step, 0)

    for j in range(3):
        red[chan * j : chan * (j + 1)] = gq[:, chan * j : chan * (j + 1)]
    red[3 * chan : 4 * chan] = gp[...]
    for j in range(4):
        red[chan * (4 + j) : chan * (5 + j)] = gu[:, chan * j : chan * (j + 1)]
        red[chan * (8 + j) : chan * (9 + j)] = gd[:, chan * j : chan * (j + 1)]
    rows = red.shape[0]
    size_c = rows // 2
    size_z = size_c // (n_x * n_z)

    def copy_to(peer, src, dst, sem):
        return pltpu.make_async_remote_copy(
            src_ref=src, dst_ref=dst, send_sem=red_ssem.at[sem], recv_sem=red_rsem.at[sem],
            device_id=peer, device_id_type=MESH,
        )

    def at(start, size):
        return pl.ds(pl.multiple_of(start, 16), size)

    red_send[...] = red[...].astype(bf16)
    sem = 0
    copies = []
    base = core * size_c
    first = copy_to(core_peer(1), red_send.at[at((1 - core) * size_c, size_c)], red_core, sem)
    first.start()
    copies.append(first)
    sem += 1
    if steps > 1:
        finish(steps - 2)
    first.wait_recv()
    red[at(base, size_c)] += red_core[...].astype(f32)

    def reduce_stage(base, size, n, index, peer, landing, sem):
        red_send2 = red_stage[len(landings)]
        landings.append(0)
        red_send2[...] = red[at(base, size * n)].astype(bf16)
        started = []
        for s in range(1, n):
            other = lax.rem(index + s, n)
            started.append(
                copy_to(peer(s), red_send2.at[at(other * size, size)], landing.at[s - 1], sem)
            )
            started[-1].start()
            sem += 1
        base = base + index * size
        for copy in started:
            copy.wait_recv()
        total = red[at(base, size)]
        for s in range(1, n):
            total += landing[s - 1].astype(f32)
        red[at(base, size)] = total
        copies.extend(started)
        return base, sem

    landings = []
    red_stage = (full.at[pl.ds(rows, size_c)],)
    base, sem = reduce_stage(base, size_z, n_x * n_z, plane_at, plane_peer, red_plane, sem)
    red_y[y_at] = red[at(base, size_z)].astype(bf16)
    started = []
    for s in range(1, n_y):
        started.append(copy_to(y_peer(s), red_y.at[y_at], red_y.at[y_at], sem))
        started[-1].start()
        sem += 1
    finish(steps - 1)
    for copy in started:
        copy.wait_recv()
    copies.extend(started)
    total = red_y[0].astype(f32)
    for j in range(1, n_y):
        total += red_y[j].astype(f32)
    full[at(base, size_z)] = total.astype(bf16)

    def gather_stage(base, size, n, peer, sem):
        started = []
        for s in range(1, n):
            part = full.at[at(base, size)]
            started.append(copy_to(peer(s), part, part, sem))
            started[-1].start()
            sem += 1
        for copy in started:
            copy.wait_recv()
        copies.extend(started)
        return sem

    sem = gather_stage(base, size_z, n_x * n_z, plane_peer, sem)
    sem = gather_stage(core * size_c, size_c, 2, core_peer, sem)
    full_out[...] = full[:rows]
    for copy in copies:
        copy.wait_send()

    def drain(s, carry):
        for copy in in_copies(s) + out_copies(s):
            copy.wait_send()
        grad_copy(s).wait()
        return carry

    lax.fori_loop(0, steps, drain, 0)


def finish_kernel(
    factor, grad_b, full, grad, g_qkv, g_proj, g_up, g_down, narrow, wide, load_sem, store_sem
):
    steps = load_sem.shape[0]
    per = narrow.shape[0] // steps
    chan = full.shape[1]

    def load(s):
        span = pl.ds(s * per, per)
        return pltpu.make_async_copy(grad_b.at[span], narrow.at[span], load_sem.at[s])

    def store(s):
        span = pl.ds(s * per, per)
        return pltpu.make_async_copy(wide.at[span], grad.at[span], store_sem.at[s])

    def block(j):
        return full[chan * j : chan * (j + 1)].astype(f32) * factor

    for s in range(steps):
        load(s).start()
    for j in range(g_qkv.shape[1] // chan):
        g_qkv[:, chan * j : chan * (j + 1)] = block(j)
    g_proj[...] = block(3)
    for j in range(g_up.shape[1] // chan):
        g_up[:, chan * j : chan * (j + 1)] = block(4 + j)
        g_down[chan * j : chan * (j + 1)] = block(8 + j).T
    for s in range(steps):
        load(s).wait()
        wide[per * s : per * (s + 1)] = narrow[per * s : per * (s + 1)].astype(f32)
        store(s).start()
    for s in range(steps):
        store(s).wait()


def solution(mesh):
    n_row, n_col = mesh.shape["row"], mesh.shape["col"]

    def shards(frames, cotangent, gain1, w_qkv, rel_bias, w_proj, gain2, w_up, w_down):
        nfr, tile_h, tile_w, chan = frames.shape
        ff = w_up.shape[1]
        factor = float(nfr * tile_h * tile_w * n_row * n_col) ** -0.5
        long, short = (tile_h - SHIFT) // 2, SHIFT // 2
        wide = WS * WS
        rows = 4 * chan + 2 * ff
        n_z, n_x = min(4, n_row), min(4, n_col // 2)
        n_y = (n_row // n_z) * (n_col // (2 * n_x))
        size_c = rows // 2
        size_z = size_c // (n_x * n_z)
        n_sem = 2 + 2 * (n_x * n_z - 1) + (n_y - 1)

        def pieces(k):
            sizes = (long, short, short)
            lead = (nfr,) if k == 1 else (nfr, k)
            return [pltpu.VMEM(lead + (n, 2 * SHIFT, chan), bf16) for n in sizes]

        vmem = pl.BlockSpec(memory_space=pltpu.VMEM)
        hbm = pl.BlockSpec(memory_space=pl.ANY)
        steps, windows = nfr // PER, tile_h // WS
        grad_b, full = pl.pallas_call(
            functools.partial(block_kernel, n_row, n_col),
            out_shape=[
                jax.ShapeDtypeStruct(frames.shape, bf16),
                jax.ShapeDtypeStruct((rows, chan), bf16),
            ],
            in_specs=[hbm, hbm, vmem, vmem, hbm, vmem, vmem, vmem, vmem],
            out_specs=[hbm, vmem],
            scratch_shapes=[
                pltpu.VMEM(frames.shape, bf16),
                pltpu.VMEM(frames.shape, bf16),
                pltpu.VMEM(rel_bias.shape, f32),
            ]
            + pieces(2) + pieces(2) + pieces(1) + pieces(1)
            + [
                pltpu.VMEM((nfr, long, 2 * SHIFT, chan), bf16),
                pltpu.VMEM(frames.shape, bf16),
                pltpu.VMEM((PER * windows, HEADS, wide, wide), bf16),
                pltpu.VMEM((PER, windows, HEADS, wide, wide), f32),
                pltpu.VMEM((chan, 3 * chan), f32),
                pltpu.VMEM((chan, chan), f32),
                pltpu.VMEM((chan, ff), f32),
                pltpu.VMEM((chan, ff), f32),
                pltpu.VMEM((rows, chan), f32),
                pltpu.VMEM((rows, chan), bf16),
                pltpu.VMEM((size_c, chan), bf16),
                pltpu.VMEM((n_x * n_z - 1, size_z, chan), bf16),
                pltpu.VMEM((n_y, size_z, chan), bf16),
                pltpu.VMEM((rows + size_c, chan), bf16),
                pltpu.SemaphoreType.DMA((2, steps + 1)),
                pltpu.SemaphoreType.DMA((3, nfr)),
                pltpu.SemaphoreType.DMA((3, nfr)),
                pltpu.SemaphoreType.DMA((3, nfr)),
                pltpu.SemaphoreType.DMA((3, nfr)),
                pltpu.SemaphoreType.DMA((steps,)),
                pltpu.SemaphoreType.DMA((n_sem,)),
                pltpu.SemaphoreType.DMA((n_sem,)),
            ],
            compiler_params=pltpu.CompilerParams(
                collective_id=0, has_side_effects=True, vmem_limit_bytes=56 * 2**20
            ),
        )(
            frames, cotangent, gain1.reshape(1, chan), w_qkv, rel_bias, w_proj,
            gain2.reshape(1, chan), w_up, w_down,
        )

        sizes = [(chan, 3 * chan), (chan, chan), (chan, ff), (ff, chan)]
        return pl.pallas_call(
            functools.partial(finish_kernel, factor),
            out_shape=[jax.ShapeDtypeStruct(frames.shape, f32)]
            + [jax.ShapeDtypeStruct(size, f32) for size in sizes],
            in_specs=[hbm, vmem],
            out_specs=[hbm] + [vmem] * 4,
            scratch_shapes=[
                pltpu.VMEM(frames.shape, bf16),
                pltpu.VMEM(frames.shape, f32),
                pltpu.SemaphoreType.DMA((steps,)),
                pltpu.SemaphoreType.DMA((steps,)),
            ],
            compiler_params=pltpu.CompilerParams(vmem_limit_bytes=56 * 2**20),
        )(grad_b, full)

    tiles = P(None, "row", "col", None)
    return jax.shard_map(
        shards,
        mesh=mesh,
        in_specs=(tiles, tiles) + (P(),) * 7,
        out_specs=(tiles, P(), P(), P(), P()),
        check_vma=False,
    )
```

```python
import functools
import math

import jax
import jax.numpy as jnp
from jax import lax
from jax.experimental import pallas as pl
from jax.experimental.pallas import tpu as pltpu
from jax.sharding import PartitionSpec as P

HEADS = 4
WS = 16
SHIFT = 8
EPS = 1e-05
LOG2E = math.log2(math.e)
MESH = pl.DeviceIdType.MESH
bf16 = jnp.bfloat16
f32 = jnp.float32
PER = 4


def dot(a, b, ca, cb):
    return lax.dot_general(a, b, (((ca,), (cb,)), ((), ())), preferred_element_type=f32)


def layer_norm_stats(x):
    centered = x - jnp.mean(x, -1, keepdims=True)
    rstd = lax.rsqrt(jnp.mean(centered * centered, -1, keepdims=True) + EPS)
    return centered * rstd, rstd


def layer_norm_backward(dy, gain, xhat, rstd):
    dxh = dy * gain
    return rstd * (
        dxh
        - jnp.mean(dxh, -1, keepdims=True)
        - xhat * jnp.mean(dxh * xhat, -1, keepdims=True)
    )


def gelu_and_slope(u):
    expo = jnp.exp2(u * u * (-0.5 * LOG2E))
    p = math.sqrt(2.0) / 0.3275911
    t = 1.0 / (jnp.abs(u) + p)
    poly = 0.5 * 1.061405429 * p**5
    for n, c in ((4, -1.453152027), (3, 1.421413741), (2, -0.284496736), (1, 0.254829592)):
        poly = t * poly + 0.5 * c * p**n
    tail = t * poly * expo
    cdf = jnp.where(u < 0.0, tail, 1.0 - tail)
    return u * cdf, cdf + u * expo * (1.0 / math.sqrt(2.0 * math.pi))


def window_block(at, x, c, bias, g1, g2, w_qkv, w_proj, w_up, w_down, probs, acc, result):
    gq, gp, gu, gd = acc
    tokens, chan = x.shape
    hd = chan // HEADS
    ff = w_up.shape[1]
    head = lax.broadcasted_iota(jnp.int32, (tokens, chan), 1) // hd
    xhat1, rstd1 = layer_norm_stats(x)
    y = (xhat1 * g1).astype(bf16)
    yield
    qkv = dot(y, w_qkv[...], 1, 0)
    yield
    q = qkv[:, :chan] * (LOG2E / math.sqrt(hd))
    k = qkv[:, chan : 2 * chan].astype(bf16)
    v_one = jnp.concatenate([qkv[:, 2 * chan :].astype(bf16), jnp.ones((tokens, chan), bf16)], 1)
    yield
    total, norm = None, None
    for h in range(HEADS):
        mine = head == h
        scores = dot(jnp.where(mine, q, 0.0).astype(bf16), k, 1, 1) + bias[h]
        yield
        expo = jnp.exp2(scores - jnp.max(scores, -1, keepdims=True)).astype(bf16)
        probs[at, h] = expo
        yield
        out = dot(expo, v_one, 1, 0)
        total = out[:, :chan] if h == 0 else jnp.where(mine, out[:, :chan], total)
        norm = out[:, chan:] if h == 0 else jnp.where(mine, out[:, chan:], norm)
        yield
    inverse = 1.0 / norm
    attended = total * inverse
    attended_b = attended.astype(bf16)
    proj = dot(attended_b, w_proj[...], 1, 0).astype(bf16)
    yield
    x1 = (x + proj.astype(f32)).astype(bf16).astype(f32)
    xhat2, rstd2 = layer_norm_stats(x1)
    z = (xhat2 * g2).astype(bf16)
    c_b = c.astype(bf16)
    yield
    z_t, c_t = z.T, c_b.T
    dz = None
    part = ff // 2
    for j in range(0, ff, part):
        u = dot(z, w_up[:, j : j + part], 1, 0)
        d_hid = dot(c_b, w_down[j : j + part, :], 1, 1)
        yield
        act, slope = gelu_and_slope(u)
        hid = act.astype(bf16)
        du = (d_hid * slope).astype(bf16)
        yield
        gd[:, j : j + part] += dot(c_t, hid, 1, 0)
        gu[:, j : j + part] += dot(z_t, du, 1, 0)
        more = dot(du, w_up[:, j : j + part], 1, 1)
        dz = more if dz is None else dz + more
        yield
    dx1 = c + layer_norm_backward(dz, g2, xhat2, rstd2)
    dx1_b = dx1.astype(bf16)
    gp[...] += dot(attended_b, dx1_b, 0, 0)
    d_att = dot(dx1_b, w_proj[...], 1, 1).astype(bf16).astype(f32)
    yield
    d_att = d_att * inverse
    d_sum = -(d_att * attended)
    q_t = q.astype(bf16).T
    d_att_t = d_att.astype(bf16).T
    yield
    dv, dk, dq = [], [], None
    for h in range(HEADS):
        mine = head == h
        left = jnp.concatenate(
            [jnp.where(mine, d_att, 0.0).astype(bf16), jnp.where(mine, d_sum, 0.0).astype(bf16)], 1
        )
        d_prob = dot(left, v_one, 1, 1)
        yield
        expo = probs[at, h]
        ds = (expo.astype(f32) * d_prob).astype(bf16)
        yield
        dv.append(dot(d_att_t[hd * h : hd * (h + 1)], expo, 1, 0))
        dk.append(dot(q_t[hd * h : hd * (h + 1)], ds, 1, 0))
        out = dot(ds, k, 1, 0)
        dq = out if h == 0 else jnp.where(mine, out, dq)
        yield
    dqkv = jnp.concatenate(
        [
            (dq * hd**-0.5).astype(bf16),
            (jnp.concatenate(dk, 0) * (1.0 / LOG2E)).astype(bf16).T,
            jnp.concatenate(dv, 0).astype(bf16).T,
        ],
        1,
    )
    yield
    gq[...] += dot(y, dqkv, 0, 0)
    d_shift = dot(dqkv, w_qkv[...], 1, 1).astype(bf16).astype(f32)
    result[at] = dx1 + layer_norm_backward(d_shift, g1, xhat1, rstd1)
    yield


def take_turns(stages):
    while stages:
        stages = [one for one in stages if next(one, stages) is not stages]


def halves(tile):
    return tile.reshape(tile.shape[0] // 2, 2 * tile.shape[1], tile.shape[2]).astype(bf16)


def unhalves(packed):
    return packed.astype(f32).reshape(packed.shape[0] * 2, packed.shape[1] // 2, packed.shape[2])


def block_kernel(
    n_row, n_col,
    frames_in, cotangent_in, gain1, w_qkv, bias_in, w_proj, gain2, w_up, w_down,
    grad, full_out,
    frames, cotangent, rel_bias,
    to_side, to_row, to_corner, from_side, from_row, from_corner,
    back_side, back_row, back_corner, got_side, got_row, got_corner,
    own_out, tile, probs, bias, gq, gp, gu, gd,
    red, red_send, red_core, red_plane, red_y, full,
    load_sem, in_send, in_recv, out_send, out_recv, grad_sem, red_ssem, red_rsem,
):
    nfr, tile_h, tile_w, chan = frames.shape
    steps = nfr // PER
    row, col = lax.axis_index("row"), lax.axis_index("col")

    def loads(s):
        span = pl.ds(s * PER, PER)
        return [
            pltpu.make_async_copy(frames_in.at[span], frames.at[span], load_sem.at[0, s]),
            pltpu.make_async_copy(cotangent_in.at[span], cotangent.at[span], load_sem.at[1, s]),
        ]

    bias_load = pltpu.make_async_copy(bias_in, rel_bias, load_sem.at[0, steps])
    for s in range(min(2, steps)):
        for copy in loads(s):
            copy.start()
    bias_load.start()
    for s in range(2, steps):
        for copy in loads(s):
            copy.start()

    n_z = min(4, n_row)
    n_yh = n_row // n_z
    n_x = min(4, n_col // 2)
    n_yl = n_col // (2 * n_x)
    n_y = n_yh * n_yl
    core, x_at, y_lo = lax.rem(col, 2), lax.rem(col // 2, n_x), col // (2 * n_x)
    z_at, y_hi = lax.rem(row, n_z), row // n_z
    y_at = y_hi * n_yl + y_lo

    left, right = lax.rem(col + n_col - 1, n_col), lax.rem(col + 1, n_col)
    up, down = lax.rem(row + n_row - 1, n_row), lax.rem(row + 1, n_row)
    ways = (((row, left), (up, col), (up, left)), ((row, right), (down, col), (down, right)))

    def core_peer(s):
        return (row, col + 1 - 2 * core)

    plane_at = z_at * n_x + x_at

    def plane_peer(s):
        other = lax.rem(plane_at + s, n_x * n_z)
        return (y_hi * n_z + other // n_x, (y_lo * n_x + lax.rem(other, n_x)) * 2 + core)

    def y_peer(s):
        other = lax.rem(y_at + s, n_y)
        return ((other // n_yl) * n_z + z_at, (lax.rem(other, n_yl) * n_x + x_at) * 2 + core)

    peers = list(ways[0]) + list(ways[1]) + [core_peer(1)]
    peers += [plane_peer(s) for s in range(1, n_x * n_z)]
    peers += [y_peer(s) for s in range(1, n_y)]
    barrier = pltpu.get_barrier_semaphore()
    for peer in peers:
        pl.semaphore_signal(barrier, inc=1, device_id=peer, device_id_type=MESH)

    def in_copies(s):
        pairs = ((to_side, from_side), (to_row, from_row), (to_corner, from_corner))
        return [
            pltpu.make_async_remote_copy(
                src_ref=a.at[s * PER + f], dst_ref=b.at[s * PER + f],
                send_sem=in_send.at[i, s * PER + f], recv_sem=in_recv.at[i, s * PER + f],
                device_id=ways[f % 2][i], device_id_type=MESH,
            )
            for f in range(PER)
            for i, (a, b) in enumerate(pairs)
        ]

    def out_copies(s):
        pairs = ((back_side, got_side), (back_row, got_row), (back_corner, got_corner))
        return [
            pltpu.make_async_remote_copy(
                src_ref=a.at[s * PER + f], dst_ref=b.at[s * PER + f],
                send_sem=out_send.at[i, s * PER + f], recv_sem=out_recv.at[i, s * PER + f],
                device_id=ways[1 - f % 2][i], device_id_type=MESH,
            )
            for f in range(PER)
            for i, (a, b) in enumerate(pairs)
        ]

    def pack_in(s):
        for copy in loads(s):
            copy.wait()
        for f in range(PER):
            at = s * PER + f
            rows_near, rows_far, cols_near, cols_far = cuts[f % 2]
            for i, source in enumerate((frames, cotangent)):
                whole = source[at].astype(f32)
                to_side[at, i] = halves(whole[rows_near, cols_far])
                to_row[at, i] = halves(whole[rows_far, cols_near])
                to_corner[at, i] = halves(whole[rows_far, cols_far])

    def send_in(s):
        pack_in(s)
        for copy in in_copies(s):
            copy.start()

    keep = tile_h - SHIFT
    cuts = (
        (slice(SHIFT, None), slice(0, SHIFT), slice(SHIFT, None), slice(0, SHIFT)),
        (slice(0, keep), slice(keep, None), slice(0, SHIFT), slice(SHIFT, None)),
    )

    def put(f, kept, side, over, corner):
        order = (lambda a, b: (a, b)) if f == 0 else (lambda a, b: (b, a))
        body = jnp.concatenate(order(kept, side), 1)
        edge = jnp.concatenate(order(over, corner), 1)
        return jnp.concatenate(order(body, edge), 0)

    def grad_copy(s):
        span = pl.ds(s * PER, PER)
        return pltpu.make_async_copy(tile.at[span], grad.at[span], grad_sem.at[s])

    def finish(s):
        for copy in out_copies(s):
            copy.wait_recv()
        for f in range(PER):
            at = s * PER + f
            parts = (own_out, got_side, got_row, got_corner)
            tile[at] = put(1 - f % 2, *(unhalves(p[at]) for p in parts)).astype(bf16)
        grad_copy(s).start()

    pack_in(0)
    pl.semaphore_wait(barrier, len(peers))
    for copy in in_copies(0):
        copy.start()

    bias_load.wait()
    wide = WS * WS
    at_q = lax.broadcasted_iota(jnp.int32, (wide, wide), 0)
    at_k = lax.broadcasted_iota(jnp.int32, (wide, wide), 1)
    cut_row = (at_q // (WS * SHIFT)) != (at_k // (WS * SHIFT))
    cut_col = (lax.rem(at_q, WS) // SHIFT) != (lax.rem(at_k, WS) // SHIFT)
    windows = tile_h // WS
    for f in range(2):
        last_row = jnp.where(row == (n_row - 1 if f == 0 else 0), 1.0, 0.0)
        last_col = jnp.where(col == (n_col - 1 if f == 0 else 0), 1.0, 0.0)
        by_row = jnp.where(cut_row, last_row, 0.0)
        by_col = jnp.where(cut_col, last_col, 0.0)
        for w in range(windows):
            at_edge = w == (windows - 1 if f == 0 else 0)
            cut = jnp.maximum(by_row, by_col) if at_edge else by_col
            for h in range(HEADS):
                bias[f, w, h] = (rel_bias[h] + cut * -100.0) * LOG2E
    for ref in (gq, gp, gu, gd):
        ref[...] = jnp.zeros_like(ref)

    def arrive(s):
        for copy in in_copies(s):
            copy.wait_recv()

    if steps > 1:
        pack_in(1)
    arrive(0)
    if steps > 1:
        for copy in in_copies(1):
            copy.start()

    def step(s, carry):
        @pl.when(s + 2 < steps)
        def _():
            send_in(s + 2)

        stages, result = [], [None] * (PER * windows)
        for f in range(PER):
            at = s * PER + f
            parts = []
            for i, source in enumerate((frames, cotangent)):
                own = source[at].astype(f32)[cuts[f % 2][0], cuts[f % 2][2]]
                got = (unhalves(p[at, i]) for p in (from_side, from_row, from_corner))
                parts.append(put(f % 2, own, *got))
            for w in range(windows):
                x, c = (p[w * WS : (w + 1) * WS].reshape(wide, chan) for p in parts)
                stages.append(
                    window_block(
                        f * windows + w, x, c, bias.at[f % 2, w], gain1[...], gain2[...],
                        w_qkv, w_proj, w_up, w_down, probs, (gq, gp, gu, gd), result,
                    )
                )
        take_turns(stages)
        for f in range(PER):
            at = s * PER + f
            out = [r.reshape(WS, WS, chan) for r in result[f * windows : (f + 1) * windows]]
            out = jnp.concatenate(out, 0)
            if f % 2 == 0:
                rows_own, rows_far = slice(0, keep), slice(keep, None)
                cols_own, cols_far = slice(0, SHIFT), slice(SHIFT, None)
            else:
                rows_own, rows_far = slice(SHIFT, None), slice(0, SHIFT)
                cols_own, cols_far = slice(SHIFT, None), slice(0, SHIFT)
            back_side[at] = halves(out[rows_own, cols_far])
            back_row[at] = halves(out[rows_far, cols_own])
            back_corner[at] = halves(out[rows_far, cols_far])
            own_out[at] = halves(out[rows_own, cols_own])
        for copy in out_copies(s):
            copy.start()

        @pl.when(s >= 2)
        def _():
            finish(s - 2)

        @pl.when(s + 1 < steps)
        def _():
            arrive(s + 1)

        return carry

    lax.fori_loop(0, steps, step, 0)

    for j in range(3):
        red[chan * j : chan * (j + 1)] = gq[:, chan * j : chan * (j + 1)]
    red[3 * chan : 4 * chan] = gp[...]
    for j in range(4):
        red[chan * (4 + j) : chan * (5 + j)] = gu[:, chan * j : chan * (j + 1)]
        red[chan * (8 + j) : chan * (9 + j)] = gd[:, chan * j : chan * (j + 1)]
    rows = red.shape[0]
    size_c = rows // 2
    size_z = size_c // (n_x * n_z)

    def copy_to(peer, src, dst, sem):
        return pltpu.make_async_remote_copy(
            src_ref=src, dst_ref=dst, send_sem=red_ssem.at[sem], recv_sem=red_rsem.at[sem],
            device_id=peer, device_id_type=MESH,
        )

    def at(start, size):
        return pl.ds(pl.multiple_of(start, 16), size)

    red_send[...] = red[...].astype(bf16)
    sem = 0
    copies = []
    base = core * size_c
    first = copy_to(core_peer(1), red_send.at[at((1 - core) * size_c, size_c)], red_core, sem)
    first.start()
    copies.append(first)
    sem += 1
    if steps > 1:
        finish(steps - 2)
    first.wait_recv()
    red[at(base, size_c)] += red_core[...].astype(f32)

    def reduce_stage(base, size, n, index, peer, landing, sem):
        red_send2 = red_stage[len(landings)]
        landings.append(0)
        red_send2[...] = red[at(base, size * n)].astype(bf16)
        started = []
        for s in range(1, n):
            other = lax.rem(index + s, n)
            started.append(
                copy_to(peer(s), red_send2.at[at(other * size, size)], landing.at[s - 1], sem)
            )
            started[-1].start()
            sem += 1
        base = base + index * size
        for copy in started:
            copy.wait_recv()
        total = red[at(base, size)]
        for s in range(1, n):
            total += landing[s - 1].astype(f32)
        red[at(base, size)] = total
        copies.extend(started)
        return base, sem

    landings = []
    red_stage = (full.at[pl.ds(rows, size_c)],)
    base, sem = reduce_stage(base, size_z, n_x * n_z, plane_at, plane_peer, red_plane, sem)
    red_y[y_at] = red[at(base, size_z)].astype(bf16)
    started = []
    for s in range(1, n_y):
        started.append(copy_to(y_peer(s), red_y.at[y_at], red_y.at[y_at], sem))
        started[-1].start()
        sem += 1
    finish(steps - 1)
    for copy in started:
        copy.wait_recv()
    copies.extend(started)
    total = red_y[0].astype(f32)
    for j in range(1, n_y):
        total += red_y[j].astype(f32)
    full[at(base, size_z)] = total.astype(bf16)

    def gather_stage(base, size, n, peer, sem):
        started = []
        for s in range(1, n):
            part = full.at[at(base, size)]
            started.append(copy_to(peer(s), part, part, sem))
            started[-1].start()
            sem += 1
        for copy in started:
            copy.wait_recv()
        copies.extend(started)
        return sem

    sem = gather_stage(base, size_z, n_x * n_z, plane_peer, sem)
    sem = gather_stage(core * size_c, size_c, 2, core_peer, sem)
    full_out[...] = full[:rows]
    for copy in copies:
        copy.wait_send()

    def drain(s, carry):
        for copy in in_copies(s) + out_copies(s):
            copy.wait_send()
        grad_copy(s).wait()
        return carry

    lax.fori_loop(0, steps, drain, 0)


def finish_kernel(
    factor, grad_b, full_in, grad, qkv_out, proj_out, up_out, down_out,
    narrow, wide, full, g_qkv, g_proj, g_up, g_down, load_sem, store_sem, full_sem, sum_sem,
):
    steps = load_sem.shape[0]
    per = narrow.shape[0] // steps
    chan = full.shape[1]

    def load(s):
        span = pl.ds(s * per, per)
        return pltpu.make_async_copy(grad_b.at[span], narrow.at[span], load_sem.at[s])

    def store(s):
        span = pl.ds(s * per, per)
        return pltpu.make_async_copy(wide.at[span], grad.at[span], store_sem.at[s])

    def block(j):
        return full[chan * j : chan * (j + 1)].astype(f32) * factor

    full_load = pltpu.make_async_copy(full_in, full, full_sem)
    for s in range(steps):
        load(s).start()
    full_load.start()
    for s in range(steps):
        load(s).wait()
        wide[per * s : per * (s + 1)] = narrow[per * s : per * (s + 1)].astype(f32)
        store(s).start()
    full_load.wait()
    for j in range(g_qkv.shape[1] // chan):
        g_qkv[:, chan * j : chan * (j + 1)] = block(j)
    g_proj[...] = block(3)
    for j in range(g_up.shape[1] // chan):
        g_up[:, chan * j : chan * (j + 1)] = block(4 + j)
        g_down[chan * j : chan * (j + 1)] = block(8 + j).T
    pairs = ((g_qkv, qkv_out), (g_proj, proj_out), (g_up, up_out), (g_down, down_out))
    sums = [pltpu.make_async_copy(a, b, sum_sem.at[i]) for i, (a, b) in enumerate(pairs)]
    for copy in sums:
        copy.start()
    for s in range(steps):
        store(s).wait()
    for copy in sums:
        copy.wait()


def solution(mesh):
    n_row, n_col = mesh.shape["row"], mesh.shape["col"]

    def shards(frames, cotangent, gain1, w_qkv, rel_bias, w_proj, gain2, w_up, w_down):
        nfr, tile_h, tile_w, chan = frames.shape
        ff = w_up.shape[1]
        factor = float(nfr * tile_h * tile_w * n_row * n_col) ** -0.5
        long, short = (tile_h - SHIFT) // 2, SHIFT // 2
        wide = WS * WS
        rows = 4 * chan + 2 * ff
        n_z, n_x = min(4, n_row), min(4, n_col // 2)
        n_y = (n_row // n_z) * (n_col // (2 * n_x))
        size_c = rows // 2
        size_z = size_c // (n_x * n_z)
        n_sem = 2 + 2 * (n_x * n_z - 1) + (n_y - 1)

        def pieces(k):
            sizes = (long, short, short)
            lead = (nfr,) if k == 1 else (nfr, k)
            return [pltpu.VMEM(lead + (n, 2 * SHIFT, chan), bf16) for n in sizes]

        vmem = pl.BlockSpec(memory_space=pltpu.VMEM)
        hbm = pl.BlockSpec(memory_space=pl.ANY)
        steps, windows = nfr // PER, tile_h // WS
        grad_b, full = pl.pallas_call(
            functools.partial(block_kernel, n_row, n_col),
            out_shape=[
                jax.ShapeDtypeStruct(frames.shape, bf16),
                jax.ShapeDtypeStruct((rows, chan), bf16),
            ],
            in_specs=[hbm, hbm, vmem, vmem, hbm, vmem, vmem, vmem, vmem],
            out_specs=[hbm, vmem],
            scratch_shapes=[
                pltpu.VMEM(frames.shape, bf16),
                pltpu.VMEM(frames.shape, bf16),
                pltpu.VMEM(rel_bias.shape, f32),
            ]
            + pieces(2) + pieces(2) + pieces(1) + pieces(1)
            + [
                pltpu.VMEM((nfr, long, 2 * SHIFT, chan), bf16),
                pltpu.VMEM(frames.shape, bf16),
                pltpu.VMEM((PER * windows, HEADS, wide, wide), bf16),
                pltpu.VMEM((2, windows, HEADS, wide, wide), f32),
                pltpu.VMEM((chan, 3 * chan), f32),
                pltpu.VMEM((chan, chan), f32),
                pltpu.VMEM((chan, ff), f32),
                pltpu.VMEM((chan, ff), f32),
                pltpu.VMEM((rows, chan), f32),
                pltpu.VMEM((rows, chan), bf16),
                pltpu.VMEM((size_c, chan), bf16),
                pltpu.VMEM((n_x * n_z - 1, size_z, chan), bf16),
                pltpu.VMEM((n_y, size_z, chan), bf16),
                pltpu.VMEM((rows + size_c, chan), bf16),
                pltpu.SemaphoreType.DMA((2, steps + 1)),
                pltpu.SemaphoreType.DMA((3, nfr)),
                pltpu.SemaphoreType.DMA((3, nfr)),
                pltpu.SemaphoreType.DMA((3, nfr)),
                pltpu.SemaphoreType.DMA((3, nfr)),
                pltpu.SemaphoreType.DMA((steps,)),
                pltpu.SemaphoreType.DMA((n_sem,)),
                pltpu.SemaphoreType.DMA((n_sem,)),
            ],
            compiler_params=pltpu.CompilerParams(
                collective_id=0, has_side_effects=True, vmem_limit_bytes=56 * 2**20
            ),
        )(
            frames, cotangent, gain1.reshape(1, chan), w_qkv, rel_bias, w_proj,
            gain2.reshape(1, chan), w_up, w_down,
        )

        sizes = [(chan, 3 * chan), (chan, chan), (chan, ff), (ff, chan)]
        return pl.pallas_call(
            functools.partial(finish_kernel, factor),
            out_shape=[jax.ShapeDtypeStruct(frames.shape, f32)]
            + [jax.ShapeDtypeStruct(size, f32) for size in sizes],
            in_specs=[hbm, hbm],
            out_specs=[hbm] * 5,
            scratch_shapes=[
                pltpu.VMEM(frames.shape, bf16),
                pltpu.VMEM(frames.shape, f32),
                pltpu.VMEM((rows, chan), bf16),
            ]
            + [pltpu.VMEM(size, f32) for size in sizes]
            + [
                pltpu.SemaphoreType.DMA((nfr // 2,)),
                pltpu.SemaphoreType.DMA((nfr // 2,)),
                pltpu.SemaphoreType.DMA,
                pltpu.SemaphoreType.DMA((4,)),
            ],
            compiler_params=pltpu.CompilerParams(vmem_limit_bytes=56 * 2**20),
        )(grad_b, full)

    tiles = P(None, "row", "col", None)
    return jax.shard_map(
        shards,
        mesh=mesh,
        in_specs=(tiles, tiles) + (P(),) * 7,
        out_specs=(tiles, P(), P(), P(), P()),
        check_vma=False,
    )
```

```python
import functools
import math

import jax
import jax.numpy as jnp
from jax import lax
from jax.experimental import pallas as pl
from jax.experimental.pallas import tpu as pltpu
from jax.sharding import PartitionSpec as P

HEADS = 4
WS = 16
SHIFT = 8
EPS = 1e-05
LOG2E = math.log2(math.e)
MESH = pl.DeviceIdType.MESH
bf16 = jnp.bfloat16
f32 = jnp.float32
PER = 4


def dot(a, b, ca, cb):
    return lax.dot_general(a, b, (((ca,), (cb,)), ((), ())), preferred_element_type=f32)


def layer_norm_stats(x):
    centered = x - jnp.mean(x, -1, keepdims=True)
    rstd = lax.rsqrt(jnp.mean(centered * centered, -1, keepdims=True) + EPS)
    return centered * rstd, rstd


def layer_norm_backward(dy, gain, xhat, rstd):
    dxh = dy * gain
    return rstd * (
        dxh
        - jnp.mean(dxh, -1, keepdims=True)
        - xhat * jnp.mean(dxh * xhat, -1, keepdims=True)
    )


def gelu_and_slope(u):
    expo = jnp.exp2(u * u * (-0.5 * LOG2E))
    p = math.sqrt(2.0) / 0.3275911
    t = 1.0 / (jnp.abs(u) + p)
    poly = 0.5 * 1.061405429 * p**5
    for n, c in ((4, -1.453152027), (3, 1.421413741), (2, -0.284496736), (1, 0.254829592)):
        poly = t * poly + 0.5 * c * p**n
    tail = t * poly * expo
    cdf = jnp.where(u < 0.0, tail, 1.0 - tail)
    return u * cdf, cdf + u * expo * (1.0 / math.sqrt(2.0 * math.pi))


def window_block(at, x, c, bias, g1, g2, w_qkv, w_proj, w_up, w_down, probs, acc, result):
    gq, gp, gu, gd = acc
    tokens, chan = x.shape
    hd = chan // HEADS
    ff = w_up.shape[1]
    head = lax.broadcasted_iota(jnp.int32, (tokens, chan), 1) // hd
    xhat1, rstd1 = layer_norm_stats(x)
    y = (xhat1 * g1).astype(bf16)
    yield
    qkv = dot(y, w_qkv[...], 1, 0)
    yield
    q = qkv[:, :chan] * (LOG2E / math.sqrt(hd))
    k = qkv[:, chan : 2 * chan].astype(bf16)
    v_one = jnp.concatenate([qkv[:, 2 * chan :].astype(bf16), jnp.ones((tokens, chan), bf16)], 1)
    yield
    total, norm = None, None
    for h in range(HEADS):
        mine = head == h
        scores = dot(jnp.where(mine, q, 0.0).astype(bf16), k, 1, 1) + bias[h]
        yield
        expo = jnp.exp2(scores - jnp.max(scores, -1, keepdims=True)).astype(bf16)
        probs[at, h] = expo
        yield
        out = dot(expo, v_one, 1, 0)
        total = out[:, :chan] if h == 0 else jnp.where(mine, out[:, :chan], total)
        norm = out[:, chan:] if h == 0 else jnp.where(mine, out[:, chan:], norm)
        yield
    inverse = 1.0 / norm
    attended = total * inverse
    attended_b = attended.astype(bf16)
    proj = dot(attended_b, w_proj[...], 1, 0).astype(bf16)
    yield
    x1 = (x + proj.astype(f32)).astype(bf16).astype(f32)
    xhat2, rstd2 = layer_norm_stats(x1)
    z = (xhat2 * g2).astype(bf16)
    c_b = c.astype(bf16)
    yield
    z_t, c_t = z.T, c_b.T
    dz = None
    part = ff // 2
    for j in range(0, ff, part):
        u = dot(z, w_up[:, j : j + part], 1, 0)
        d_hid = dot(c_b, w_down[j : j + part, :], 1, 1)
        yield
        act, slope = gelu_and_slope(u)
        hid = act.astype(bf16)
        du = (d_hid * slope).astype(bf16)
        yield
        gd[:, j : j + part] += dot(c_t, hid, 1, 0)
        gu[:, j : j + part] += dot(z_t, du, 1, 0)
        more = dot(du, w_up[:, j : j + part], 1, 1)
        dz = more if dz is None else dz + more
        yield
    dx1 = c + layer_norm_backward(dz, g2, xhat2, rstd2)
    dx1_b = dx1.astype(bf16)
    gp[...] += dot(attended_b, dx1_b, 0, 0)
    d_att = dot(dx1_b, w_proj[...], 1, 1).astype(bf16).astype(f32)
    yield
    d_att = d_att * inverse
    d_sum = -(d_att * attended)
    q_t = q.astype(bf16).T
    d_att_t = d_att.astype(bf16).T
    yield
    dv, dk, dq = [], [], None
    for h in range(HEADS):
        mine = head == h
        left = jnp.concatenate(
            [jnp.where(mine, d_att, 0.0).astype(bf16), jnp.where(mine, d_sum, 0.0).astype(bf16)], 1
        )
        d_prob = dot(left, v_one, 1, 1)
        yield
        expo = probs[at, h]
        ds = (expo.astype(f32) * d_prob).astype(bf16)
        yield
        dv.append(dot(d_att_t[hd * h : hd * (h + 1)], expo, 1, 0))
        dk.append(dot(q_t[hd * h : hd * (h + 1)], ds, 1, 0))
        out = dot(ds, k, 1, 0)
        dq = out if h == 0 else jnp.where(mine, out, dq)
        yield
    dqkv = jnp.concatenate(
        [
            (dq * hd**-0.5).astype(bf16),
            (jnp.concatenate(dk, 0) * (1.0 / LOG2E)).astype(bf16).T,
            jnp.concatenate(dv, 0).astype(bf16).T,
        ],
        1,
    )
    yield
    gq[...] += dot(y, dqkv, 0, 0)
    d_shift = dot(dqkv, w_qkv[...], 1, 1).astype(bf16).astype(f32)
    result[at] = dx1 + layer_norm_backward(d_shift, g1, xhat1, rstd1)
    yield


def take_turns(stages):
    waiting, running = list(stages), []
    while waiting or running:
        if waiting:
            running.append(waiting.pop(0))
        running = [one for one in running if next(one, running) is not running]


def halves(tile):
    return tile.reshape(tile.shape[0] // 2, 2 * tile.shape[1], tile.shape[2]).astype(bf16)


def unhalves(packed):
    return packed.astype(f32).reshape(packed.shape[0] * 2, packed.shape[1] // 2, packed.shape[2])


def block_kernel(
    n_row, n_col,
    frames_in, cotangent_in, gain1, w_qkv, bias_in, w_proj, gain2, w_up, w_down,
    grad, full_out,
    frames, cotangent, rel_bias,
    to_side, to_row, to_corner, from_side, from_row, from_corner,
    back_side, back_row, back_corner, got_side, got_row, got_corner,
    own_out, tile, probs, bias, gq, gp, gu, gd,
    red, red_send, red_core, red_plane, red_y, full,
    load_sem, in_send, in_recv, out_send, out_recv, grad_sem, red_ssem, red_rsem,
):
    nfr, tile_h, tile_w, chan = frames.shape
    steps = nfr // PER
    row, col = lax.axis_index("row"), lax.axis_index("col")

    def loads(s):
        span = pl.ds(s * PER, PER)
        return [
            pltpu.make_async_copy(frames_in.at[span], frames.at[span], load_sem.at[0, s]),
            pltpu.make_async_copy(cotangent_in.at[span], cotangent.at[span], load_sem.at[1, s]),
        ]

    bias_load = pltpu.make_async_copy(bias_in, rel_bias, load_sem.at[0, steps])
    for s in range(min(2, steps)):
        for copy in loads(s):
            copy.start()
    bias_load.start()
    for s in range(2, steps):
        for copy in loads(s):
            copy.start()

    n_z = min(4, n_row)
    n_yh = n_row // n_z
    n_x = min(4, n_col // 2)
    n_yl = n_col // (2 * n_x)
    n_y = n_yh * n_yl
    core, x_at, y_lo = lax.rem(col, 2), lax.rem(col // 2, n_x), col // (2 * n_x)
    z_at, y_hi = lax.rem(row, n_z), row // n_z
    y_at = y_hi * n_yl + y_lo

    left, right = lax.rem(col + n_col - 1, n_col), lax.rem(col + 1, n_col)
    up, down = lax.rem(row + n_row - 1, n_row), lax.rem(row + 1, n_row)
    ways = (((row, left), (up, col), (up, left)), ((row, right), (down, col), (down, right)))

    def core_peer(s):
        return (row, col + 1 - 2 * core)

    plane_at = z_at * n_x + x_at

    def plane_peer(s):
        other = lax.rem(plane_at + s, n_x * n_z)
        return (y_hi * n_z + other // n_x, (y_lo * n_x + lax.rem(other, n_x)) * 2 + core)

    def y_peer(s):
        other = lax.rem(y_at + s, n_y)
        return ((other // n_yl) * n_z + z_at, (lax.rem(other, n_yl) * n_x + x_at) * 2 + core)

    peers = list(ways[0]) + list(ways[1]) + [core_peer(1)]
    peers += [plane_peer(s) for s in range(1, n_x * n_z)]
    peers += [y_peer(s) for s in range(1, n_y)]
    barrier = pltpu.get_barrier_semaphore()
    for peer in peers:
        pl.semaphore_signal(barrier, inc=1, device_id=peer, device_id_type=MESH)

    def in_copies(s):
        pairs = ((to_side, from_side), (to_row, from_row), (to_corner, from_corner))
        return [
            pltpu.make_async_remote_copy(
                src_ref=a.at[s * PER + f], dst_ref=b.at[s * PER + f],
                send_sem=in_send.at[i, s * PER + f], recv_sem=in_recv.at[i, s * PER + f],
                device_id=ways[f % 2][i], device_id_type=MESH,
            )
            for f in range(PER)
            for i, (a, b) in enumerate(pairs)
        ]

    def out_copies(s):
        pairs = ((back_side, got_side), (back_row, got_row), (back_corner, got_corner))
        return [
            pltpu.make_async_remote_copy(
                src_ref=a.at[s * PER + f], dst_ref=b.at[s * PER + f],
                send_sem=out_send.at[i, s * PER + f], recv_sem=out_recv.at[i, s * PER + f],
                device_id=ways[1 - f % 2][i], device_id_type=MESH,
            )
            for f in range(PER)
            for i, (a, b) in enumerate(pairs)
        ]

    def pack_in(s):
        for copy in loads(s):
            copy.wait()
        for f in range(PER):
            at = s * PER + f
            rows_near, rows_far, cols_near, cols_far = cuts[f % 2]
            for i, source in enumerate((frames, cotangent)):
                whole = source[at].astype(f32)
                to_side[at, i] = halves(whole[rows_near, cols_far])
                to_row[at, i] = halves(whole[rows_far, cols_near])
                to_corner[at, i] = halves(whole[rows_far, cols_far])

    def send_in(s):
        pack_in(s)
        for copy in reversed(in_copies(s)):
            copy.start()

    keep = tile_h - SHIFT
    cuts = (
        (slice(SHIFT, None), slice(0, SHIFT), slice(SHIFT, None), slice(0, SHIFT)),
        (slice(0, keep), slice(keep, None), slice(0, SHIFT), slice(SHIFT, None)),
    )

    def put(f, kept, side, over, corner):
        order = (lambda a, b: (a, b)) if f == 0 else (lambda a, b: (b, a))
        body = jnp.concatenate(order(kept, side), 1)
        edge = jnp.concatenate(order(over, corner), 1)
        return jnp.concatenate(order(body, edge), 0)

    def grad_copy(s):
        span = pl.ds(s * PER, PER)
        return pltpu.make_async_copy(tile.at[span], grad.at[span], grad_sem.at[s])

    def finish(s):
        for copy in out_copies(s):
            copy.wait_recv()
        for f in range(PER):
            at = s * PER + f
            parts = (own_out, got_side, got_row, got_corner)
            tile[at] = put(1 - f % 2, *(unhalves(p[at]) for p in parts)).astype(bf16)
        grad_copy(s).start()

    pack_in(0)
    pl.semaphore_wait(barrier, len(peers))
    for copy in reversed(in_copies(0)):
        copy.start()

    bias_load.wait()
    wide = WS * WS
    at_q = lax.broadcasted_iota(jnp.int32, (wide, wide), 0)
    at_k = lax.broadcasted_iota(jnp.int32, (wide, wide), 1)
    cut_row = (at_q // (WS * SHIFT)) != (at_k // (WS * SHIFT))
    cut_col = (lax.rem(at_q, WS) // SHIFT) != (lax.rem(at_k, WS) // SHIFT)
    windows = tile_h // WS
    for f in range(2):
        last_row = jnp.where(row == (n_row - 1 if f == 0 else 0), 1.0, 0.0)
        last_col = jnp.where(col == (n_col - 1 if f == 0 else 0), 1.0, 0.0)
        by_row = jnp.where(cut_row, last_row, 0.0)
        by_col = jnp.where(cut_col, last_col, 0.0)
        for w in range(windows):
            at_edge = w == (windows - 1 if f == 0 else 0)
            cut = jnp.maximum(by_row, by_col) if at_edge else by_col
            for h in range(HEADS):
                bias[f, w, h] = (rel_bias[h] + cut * -100.0) * LOG2E
    for ref in (gq, gp, gu, gd):
        ref[...] = jnp.zeros_like(ref)

    def arrive(s):
        for copy in in_copies(s):
            copy.wait_recv()

    if steps > 1:
        pack_in(1)
    arrive(0)
    if steps > 1:
        for copy in reversed(in_copies(1)):
            copy.start()

    def step(s, carry):
        @pl.when(s + 2 < steps)
        def _():
            send_in(s + 2)

        stages, result = [], [None] * (PER * windows)
        for f in range(PER):
            at = s * PER + f
            parts = []
            for i, source in enumerate((frames, cotangent)):
                own = source[at].astype(f32)[cuts[f % 2][0], cuts[f % 2][2]]
                got = (unhalves(p[at, i]) for p in (from_side, from_row, from_corner))
                parts.append(put(f % 2, own, *got))
            for w in range(windows):
                x, c = (p[w * WS : (w + 1) * WS].reshape(wide, chan) for p in parts)
                stages.append(
                    window_block(
                        f * windows + w, x, c, bias.at[f % 2, w], gain1[...], gain2[...],
                        w_qkv, w_proj, w_up, w_down, probs, (gq, gp, gu, gd), result,
                    )
                )
        take_turns(stages)
        for f in range(PER):
            at = s * PER + f
            out = [r.reshape(WS, WS, chan) for r in result[f * windows : (f + 1) * windows]]
            out = jnp.concatenate(out, 0)
            if f % 2 == 0:
                rows_own, rows_far = slice(0, keep), slice(keep, None)
                cols_own, cols_far = slice(0, SHIFT), slice(SHIFT, None)
            else:
                rows_own, rows_far = slice(SHIFT, None), slice(0, SHIFT)
                cols_own, cols_far = slice(SHIFT, None), slice(0, SHIFT)
            back_side[at] = halves(out[rows_own, cols_far])
            back_row[at] = halves(out[rows_far, cols_own])
            back_corner[at] = halves(out[rows_far, cols_far])
            own_out[at] = halves(out[rows_own, cols_own])
        for copy in reversed(out_copies(s)):
            copy.start()

        @pl.when(s >= 2)
        def _():
            finish(s - 2)

        @pl.when(s + 1 < steps)
        def _():
            arrive(s + 1)

        return carry

    lax.fori_loop(0, steps, step, 0)

    for j in range(3):
        red[chan * j : chan * (j + 1)] = gq[:, chan * j : chan * (j + 1)]
    red[3 * chan : 4 * chan] = gp[...]
    for j in range(4):
        red[chan * (4 + j) : chan * (5 + j)] = gu[:, chan * j : chan * (j + 1)]
        red[chan * (8 + j) : chan * (9 + j)] = gd[:, chan * j : chan * (j + 1)]
    rows = red.shape[0]
    size_c = rows // 2
    size_z = size_c // (n_x * n_z)

    def copy_to(peer, src, dst, sem):
        return pltpu.make_async_remote_copy(
            src_ref=src, dst_ref=dst, send_sem=red_ssem.at[sem], recv_sem=red_rsem.at[sem],
            device_id=peer, device_id_type=MESH,
        )

    def at(start, size):
        return pl.ds(pl.multiple_of(start, 16), size)

    red_send[...] = red[...].astype(bf16)
    sem = 0
    copies = []
    base = core * size_c
    first = copy_to(core_peer(1), red_send.at[at((1 - core) * size_c, size_c)], red_core, sem)
    first.start()
    copies.append(first)
    sem += 1
    if steps > 1:
        finish(steps - 2)
    first.wait_recv()
    red[at(base, size_c)] += red_core[...].astype(f32)

    def reduce_stage(base, size, n, index, peer, landing, sem):
        red_send2 = red_stage[len(landings)]
        landings.append(0)
        red_send2[...] = red[at(base, size * n)].astype(bf16)
        started = []
        for s in range(1, n):
            other = lax.rem(index + s, n)
            started.append(
                copy_to(peer(s), red_send2.at[at(other * size, size)], landing.at[s - 1], sem)
            )
            started[-1].start()
            sem += 1
        base = base + index * size
        for copy in started:
            copy.wait_recv()
        total = red[at(base, size)]
        for s in range(1, n):
            total += landing[s - 1].astype(f32)
        red[at(base, size)] = total
        copies.extend(started)
        return base, sem

    landings = []
    red_stage = (full.at[pl.ds(rows, size_c)],)
    base, sem = reduce_stage(base, size_z, n_x * n_z, plane_at, plane_peer, red_plane, sem)
    red_y[y_at] = red[at(base, size_z)].astype(bf16)
    started = []
    for s in range(1, n_y):
        started.append(copy_to(y_peer(s), red_y.at[y_at], red_y.at[y_at], sem))
        started[-1].start()
        sem += 1
    finish(steps - 1)
    for copy in started:
        copy.wait_recv()
    copies.extend(started)
    total = red_y[0].astype(f32)
    for j in range(1, n_y):
        total += red_y[j].astype(f32)
    full[at(base, size_z)] = total.astype(bf16)

    def gather_stage(base, size, n, peer, sem):
        started = []
        for s in range(1, n):
            part = full.at[at(base, size)]
            started.append(copy_to(peer(s), part, part, sem))
            started[-1].start()
            sem += 1
        for copy in started:
            copy.wait_recv()
        copies.extend(started)
        return sem

    sem = gather_stage(base, size_z, n_x * n_z, plane_peer, sem)
    sem = gather_stage(core * size_c, size_c, 2, core_peer, sem)
    full_out[...] = full[:rows]
    for copy in copies:
        copy.wait_send()

    def drain(s, carry):
        for copy in in_copies(s) + out_copies(s):
            copy.wait_send()
        grad_copy(s).wait()
        return carry

    lax.fori_loop(0, steps, drain, 0)


def finish_kernel(
    factor, grad_b, full_in, grad, qkv_out, proj_out, up_out, down_out,
    narrow, wide, full, g_qkv, g_proj, g_up, g_down, load_sem, store_sem, full_sem, sum_sem,
):
    steps = load_sem.shape[0]
    per = narrow.shape[0] // steps
    chan = full.shape[1]

    def load(s):
        span = pl.ds(s * per, per)
        return pltpu.make_async_copy(grad_b.at[span], narrow.at[span], load_sem.at[s])

    def store(s):
        span = pl.ds(s * per, per)
        return pltpu.make_async_copy(wide.at[span], grad.at[span], store_sem.at[s])

    def block(j):
        return full[chan * j : chan * (j + 1)].astype(f32) * factor

    full_load = pltpu.make_async_copy(full_in, full, full_sem)
    for s in range(steps):
        load(s).start()
    full_load.start()
    for s in range(steps):
        load(s).wait()
        wide[per * s : per * (s + 1)] = narrow[per * s : per * (s + 1)].astype(f32)
        store(s).start()
    full_load.wait()
    for j in range(g_qkv.shape[1] // chan):
        g_qkv[:, chan * j : chan * (j + 1)] = block(j)
    g_proj[...] = block(3)
    for j in range(g_up.shape[1] // chan):
        g_up[:, chan * j : chan * (j + 1)] = block(4 + j)
        g_down[chan * j : chan * (j + 1)] = block(8 + j).T
    pairs = ((g_qkv, qkv_out), (g_proj, proj_out), (g_up, up_out), (g_down, down_out))
    sums = [pltpu.make_async_copy(a, b, sum_sem.at[i]) for i, (a, b) in enumerate(pairs)]
    for copy in sums:
        copy.start()
    for s in range(steps):
        store(s).wait()
    for copy in sums:
        copy.wait()


def solution(mesh):
    n_row, n_col = mesh.shape["row"], mesh.shape["col"]

    def shards(frames, cotangent, gain1, w_qkv, rel_bias, w_proj, gain2, w_up, w_down):
        nfr, tile_h, tile_w, chan = frames.shape
        ff = w_up.shape[1]
        factor = float(nfr * tile_h * tile_w * n_row * n_col) ** -0.5
        long, short = (tile_h - SHIFT) // 2, SHIFT // 2
        wide = WS * WS
        rows = 4 * chan + 2 * ff
        n_z, n_x = min(4, n_row), min(4, n_col // 2)
        n_y = (n_row // n_z) * (n_col // (2 * n_x))
        size_c = rows // 2
        size_z = size_c // (n_x * n_z)
        n_sem = 2 + 2 * (n_x * n_z - 1) + (n_y - 1)

        def pieces(k):
            sizes = (long, short, short)
            lead = (nfr,) if k == 1 else (nfr, k)
            return [pltpu.VMEM(lead + (n, 2 * SHIFT, chan), bf16) for n in sizes]

        vmem = pl.BlockSpec(memory_space=pltpu.VMEM)
        hbm = pl.BlockSpec(memory_space=pl.ANY)
        steps, windows = nfr // PER, tile_h // WS
        grad_b, full = pl.pallas_call(
            functools.partial(block_kernel, n_row, n_col),
            out_shape=[
                jax.ShapeDtypeStruct(frames.shape, bf16),
                jax.ShapeDtypeStruct((rows, chan), bf16),
            ],
            in_specs=[hbm, hbm, vmem, vmem, hbm, vmem, vmem, vmem, vmem],
            out_specs=[hbm, vmem],
            scratch_shapes=[
                pltpu.VMEM(frames.shape, bf16),
                pltpu.VMEM(frames.shape, bf16),
                pltpu.VMEM(rel_bias.shape, f32),
            ]
            + pieces(2) + pieces(2) + pieces(1) + pieces(1)
            + [
                pltpu.VMEM((nfr, long, 2 * SHIFT, chan), bf16),
                pltpu.VMEM(frames.shape, bf16),
                pltpu.VMEM((PER * windows, HEADS, wide, wide), bf16),
                pltpu.VMEM((2, windows, HEADS, wide, wide), f32),
                pltpu.VMEM((chan, 3 * chan), f32),
                pltpu.VMEM((chan, chan), f32),
                pltpu.VMEM((chan, ff), f32),
                pltpu.VMEM((chan, ff), f32),
                pltpu.VMEM((rows, chan), f32),
                pltpu.VMEM((rows, chan), bf16),
                pltpu.VMEM((size_c, chan), bf16),
                pltpu.VMEM((n_x * n_z - 1, size_z, chan), bf16),
                pltpu.VMEM((n_y, size_z, chan), bf16),
                pltpu.VMEM((rows + size_c, chan), bf16),
                pltpu.SemaphoreType.DMA((2, steps + 1)),
                pltpu.SemaphoreType.DMA((3, nfr)),
                pltpu.SemaphoreType.DMA((3, nfr)),
                pltpu.SemaphoreType.DMA((3, nfr)),
                pltpu.SemaphoreType.DMA((3, nfr)),
                pltpu.SemaphoreType.DMA((steps,)),
                pltpu.SemaphoreType.DMA((n_sem,)),
                pltpu.SemaphoreType.DMA((n_sem,)),
            ],
            compiler_params=pltpu.CompilerParams(
                collective_id=0, has_side_effects=True, vmem_limit_bytes=56 * 2**20
            ),
        )(
            frames, cotangent, gain1.reshape(1, chan), w_qkv, rel_bias, w_proj,
            gain2.reshape(1, chan), w_up, w_down,
        )

        sizes = [(chan, 3 * chan), (chan, chan), (chan, ff), (ff, chan)]
        return pl.pallas_call(
            functools.partial(finish_kernel, factor),
            out_shape=[jax.ShapeDtypeStruct(frames.shape, f32)]
            + [jax.ShapeDtypeStruct(size, f32) for size in sizes],
            in_specs=[hbm, hbm],
            out_specs=[hbm] * 5,
            scratch_shapes=[
                pltpu.VMEM(frames.shape, bf16),
                pltpu.VMEM(frames.shape, f32),
                pltpu.VMEM((rows, chan), bf16),
            ]
            + [pltpu.VMEM(size, f32) for size in sizes]
            + [
                pltpu.SemaphoreType.DMA((nfr // 2,)),
                pltpu.SemaphoreType.DMA((nfr // 2,)),
                pltpu.SemaphoreType.DMA,
                pltpu.SemaphoreType.DMA((4,)),
            ],
            compiler_params=pltpu.CompilerParams(vmem_limit_bytes=56 * 2**20),
        )(grad_b, full)

    tiles = P(None, "row", "col", None)
    return jax.shard_map(
        shards,
        mesh=mesh,
        in_specs=(tiles, tiles) + (P(),) * 7,
        out_specs=(tiles, P(), P(), P(), P()),
        check_vma=False,
    )
```

```python
import functools
import math

import jax
import jax.numpy as jnp
from jax import lax
from jax.experimental import pallas as pl
from jax.experimental.pallas import tpu as pltpu
from jax.sharding import PartitionSpec as P

HEADS = 4
WS = 16
SHIFT = 8
EPS = 1e-05
LOG2E = math.log2(math.e)
MESH = pl.DeviceIdType.MESH
bf16 = jnp.bfloat16
f32 = jnp.float32
PER = 4


def dot(a, b, ca, cb):
    return lax.dot_general(a, b, (((ca,), (cb,)), ((), ())), preferred_element_type=f32)


def layer_norm_stats(x):
    centered = x - jnp.mean(x, -1, keepdims=True)
    rstd = lax.rsqrt(jnp.mean(centered * centered, -1, keepdims=True) + EPS)
    return centered * rstd, rstd


def layer_norm_backward(dy, gain, xhat, rstd):
    dxh = dy * gain
    return rstd * (
        dxh
        - jnp.mean(dxh, -1, keepdims=True)
        - xhat * jnp.mean(dxh * xhat, -1, keepdims=True)
    )


def gelu_and_slope(u):
    expo = jnp.exp2(u * u * (-0.5 * LOG2E))
    p = math.sqrt(2.0) / 0.3275911
    t = 1.0 / (jnp.abs(u) + p)
    poly = 0.5 * 1.061405429 * p**5
    for n, c in ((4, -1.453152027), (3, 1.421413741), (2, -0.284496736), (1, 0.254829592)):
        poly = t * poly + 0.5 * c * p**n
    tail = t * poly * expo
    cdf = jnp.where(u < 0.0, tail, 1.0 - tail)
    return u * cdf, cdf + u * expo * (1.0 / math.sqrt(2.0 * math.pi))


def window_block(at, x, c, bias, g1, g2, w_qkv, w_proj, w_up, w_down, probs, acc, result):
    gq, gp, gu, gd = acc
    tokens, chan = x.shape
    hd = chan // HEADS
    ff = w_up.shape[1]
    head = lax.broadcasted_iota(jnp.int32, (tokens, chan), 1) // hd
    xhat1, rstd1 = layer_norm_stats(x)
    y = (xhat1 * g1).astype(bf16)
    yield
    qkv = dot(y, w_qkv[...], 1, 0)
    yield
    q = qkv[:, :chan] * (LOG2E / math.sqrt(hd))
    k = qkv[:, chan : 2 * chan].astype(bf16)
    v_one = jnp.concatenate([qkv[:, 2 * chan :].astype(bf16), jnp.ones((tokens, chan), bf16)], 1)
    yield
    total, norm = None, None
    for h in range(HEADS):
        mine = head == h
        scores = dot(jnp.where(mine, q, 0.0).astype(bf16), k, 1, 1) + bias[h]
        yield
        expo = jnp.exp2(scores - jnp.max(scores, -1, keepdims=True)).astype(bf16)
        probs[at, h] = expo
        yield
        out = dot(expo, v_one, 1, 0)
        total = out[:, :chan] if h == 0 else jnp.where(mine, out[:, :chan], total)
        norm = out[:, chan:] if h == 0 else jnp.where(mine, out[:, chan:], norm)
        yield
    inverse = 1.0 / norm
    attended = total * inverse
    attended_b = attended.astype(bf16)
    proj = dot(attended_b, w_proj[...], 1, 0).astype(bf16)
    yield
    x1 = (x + proj.astype(f32)).astype(bf16).astype(f32)
    xhat2, rstd2 = layer_norm_stats(x1)
    z = (xhat2 * g2).astype(bf16)
    c_b = c.astype(bf16)
    yield
    z_t, c_t = z.T, c_b.T
    dz = None
    part = ff // 2
    for j in range(0, ff, part):
        u = dot(z, w_up[:, j : j + part], 1, 0)
        d_hid = dot(c_b, w_down[j : j + part, :], 1, 1)
        yield
        act, slope = gelu_and_slope(u)
        hid = act.astype(bf16)
        du = (d_hid * slope).astype(bf16)
        yield
        gd[:, j : j + part] += dot(c_t, hid, 1, 0)
        gu[:, j : j + part] += dot(z_t, du, 1, 0)
        more = dot(du, w_up[:, j : j + part], 1, 1)
        dz = more if dz is None else dz + more
        yield
    dx1 = c + layer_norm_backward(dz, g2, xhat2, rstd2)
    dx1_b = dx1.astype(bf16)
    gp[...] += dot(attended_b, dx1_b, 0, 0)
    d_att = dot(dx1_b, w_proj[...], 1, 1).astype(bf16).astype(f32)
    yield
    d_att = d_att * inverse
    d_sum = -(d_att * attended)
    q_t = q.astype(bf16).T
    d_att_t = d_att.astype(bf16).T
    yield
    dv, dk, dq = [], [], None
    for h in range(HEADS):
        mine = head == h
        left = jnp.concatenate(
            [jnp.where(mine, d_att, 0.0).astype(bf16), jnp.where(mine, d_sum, 0.0).astype(bf16)], 1
        )
        d_prob = dot(left, v_one, 1, 1)
        yield
        expo = probs[at, h]
        ds = (expo.astype(f32) * d_prob).astype(bf16)
        yield
        dv.append(dot(d_att_t[hd * h : hd * (h + 1)], expo, 1, 0))
        dk.append(dot(q_t[hd * h : hd * (h + 1)], ds, 1, 0))
        out = dot(ds, k, 1, 0)
        dq = out if h == 0 else jnp.where(mine, out, dq)
        yield
    dqkv = jnp.concatenate(
        [
            (dq * hd**-0.5).astype(bf16),
            (jnp.concatenate(dk, 0) * (1.0 / LOG2E)).astype(bf16).T,
            jnp.concatenate(dv, 0).astype(bf16).T,
        ],
        1,
    )
    yield
    gq[...] += dot(y, dqkv, 0, 0)
    d_shift = dot(dqkv, w_qkv[...], 1, 1).astype(bf16).astype(f32)
    result[at] = dx1 + layer_norm_backward(d_shift, g1, xhat1, rstd1)
    yield


def take_turns(stages):
    waiting, running = list(stages), []
    while waiting or running:
        if waiting:
            running.append(waiting.pop(0))
        running = [one for one in running if next(one, running) is not running]


def halves(tile):
    return tile.reshape(tile.shape[0] // 2, 2 * tile.shape[1], tile.shape[2]).astype(bf16)


def unhalves(packed):
    return packed.astype(f32).reshape(packed.shape[0] * 2, packed.shape[1] // 2, packed.shape[2])


def block_kernel(
    n_row, n_col,
    frames_in, cotangent_in, gain1, w_qkv, bias_in, w_proj, gain2, w_up, w_down,
    grad, full_out,
    frames, cotangent, rel_bias,
    to_side, to_row, to_corner, from_side, from_row, from_corner,
    back_side, back_row, back_corner, got_side, got_row, got_corner,
    own_out, tile, probs, bias, gq, gp, gu, gd,
    red, red_send, red_core, red_plane, red_y, full,
    load_sem, in_send, in_recv, out_send, out_recv, grad_sem, red_ssem, red_rsem,
):
    nfr, tile_h, tile_w, chan = frames.shape
    steps = nfr // PER
    row, col = lax.axis_index("row"), lax.axis_index("col")

    def loads(s):
        span = pl.ds(s * PER, PER)
        return [
            pltpu.make_async_copy(frames_in.at[span], frames.at[span], load_sem.at[0, s]),
            pltpu.make_async_copy(cotangent_in.at[span], cotangent.at[span], load_sem.at[1, s]),
        ]

    bias_load = pltpu.make_async_copy(bias_in, rel_bias, load_sem.at[0, steps])
    for s in range(min(2, steps)):
        for copy in loads(s):
            copy.start()
    bias_load.start()
    for s in range(2, steps):
        for copy in loads(s):
            copy.start()

    n_z = min(4, n_row)
    n_yh = n_row // n_z
    n_x = min(4, n_col // 2)
    n_yl = n_col // (2 * n_x)
    n_y = n_yh * n_yl
    core, x_at, y_lo = lax.rem(col, 2), lax.rem(col // 2, n_x), col // (2 * n_x)
    z_at, y_hi = lax.rem(row, n_z), row // n_z
    y_at = y_hi * n_yl + y_lo

    left, right = lax.rem(col + n_col - 1, n_col), lax.rem(col + 1, n_col)
    up, down = lax.rem(row + n_row - 1, n_row), lax.rem(row + 1, n_row)
    ways = (((row, left), (up, col), (up, left)), ((row, right), (down, col), (down, right)))

    def core_peer(s):
        return (row, col + 1 - 2 * core)

    plane_at = z_at * n_x + x_at

    def plane_peer(s):
        other = lax.rem(plane_at + s, n_x * n_z)
        return (y_hi * n_z + other // n_x, (y_lo * n_x + lax.rem(other, n_x)) * 2 + core)

    def y_peer(s):
        other = lax.rem(y_at + s, n_y)
        return ((other // n_yl) * n_z + z_at, (lax.rem(other, n_yl) * n_x + x_at) * 2 + core)

    peers = list(ways[0]) + list(ways[1]) + [core_peer(1)]
    peers += [plane_peer(s) for s in range(1, n_x * n_z)]
    peers += [y_peer(s) for s in range(1, n_y)]
    barrier = pltpu.get_barrier_semaphore()
    for peer in peers:
        pl.semaphore_signal(barrier, inc=1, device_id=peer, device_id_type=MESH)

    def in_copies(s):
        pairs = ((to_side, from_side), (to_row, from_row), (to_corner, from_corner))
        return [
            pltpu.make_async_remote_copy(
                src_ref=a.at[s * PER + f], dst_ref=b.at[s * PER + f],
                send_sem=in_send.at[i, s * PER + f], recv_sem=in_recv.at[i, s * PER + f],
                device_id=ways[f % 2][i], device_id_type=MESH,
            )
            for f in range(PER)
            for i, (a, b) in enumerate(pairs)
        ]

    def out_copies(s):
        pairs = ((back_side, got_side), (back_row, got_row), (back_corner, got_corner))
        return [
            pltpu.make_async_remote_copy(
                src_ref=a.at[s * PER + f], dst_ref=b.at[s * PER + f],
                send_sem=out_send.at[i, s * PER + f], recv_sem=out_recv.at[i, s * PER + f],
                device_id=ways[1 - f % 2][i], device_id_type=MESH,
            )
            for f in range(PER)
            for i, (a, b) in enumerate(pairs)
        ]

    def pack_in(s):
        for copy in loads(s):
            copy.wait()
        for f in range(PER):
            at = s * PER + f
            rows_near, rows_far, cols_near, cols_far = cuts[f % 2]
            for i, source in enumerate((frames, cotangent)):
                whole = source[at].astype(f32)
                to_side[at, i] = halves(whole[rows_near, cols_far])
                to_row[at, i] = halves(whole[rows_far, cols_near])
                to_corner[at, i] = halves(whole[rows_far, cols_far])

    def send_in(s):
        pack_in(s)
        for copy in reversed(in_copies(s)):
            copy.start()

    keep = tile_h - SHIFT
    cuts = (
        (slice(SHIFT, None), slice(0, SHIFT), slice(SHIFT, None), slice(0, SHIFT)),
        (slice(0, keep), slice(keep, None), slice(0, SHIFT), slice(SHIFT, None)),
    )

    def put(f, kept, side, over, corner):
        order = (lambda a, b: (a, b)) if f == 0 else (lambda a, b: (b, a))
        body = jnp.concatenate(order(kept, side), 1)
        edge = jnp.concatenate(order(over, corner), 1)
        return jnp.concatenate(order(body, edge), 0)

    def grad_copy(s):
        span = pl.ds(s * PER, PER)
        return pltpu.make_async_copy(tile.at[span], grad.at[span], grad_sem.at[s])

    def finish(s):
        for copy in out_copies(s):
            copy.wait_recv()
        for f in range(PER):
            at = s * PER + f
            parts = (own_out, got_side, got_row, got_corner)
            tile[at] = put(1 - f % 2, *(unhalves(p[at]) for p in parts)).astype(bf16)
        grad_copy(s).start()

    pack_in(0)
    pl.semaphore_wait(barrier, len(peers))
    for copy in reversed(in_copies(0)):
        copy.start()

    bias_load.wait()
    wide = WS * WS
    at_q = lax.broadcasted_iota(jnp.int32, (wide, wide), 0)
    at_k = lax.broadcasted_iota(jnp.int32, (wide, wide), 1)
    cut_row = (at_q // (WS * SHIFT)) != (at_k // (WS * SHIFT))
    cut_col = (lax.rem(at_q, WS) // SHIFT) != (lax.rem(at_k, WS) // SHIFT)
    windows = tile_h // WS
    for f in range(2):
        last_row = jnp.where(row == (n_row - 1 if f == 0 else 0), 1.0, 0.0)
        last_col = jnp.where(col == (n_col - 1 if f == 0 else 0), 1.0, 0.0)
        by_row = jnp.where(cut_row, last_row, 0.0)
        by_col = jnp.where(cut_col, last_col, 0.0)
        for w in range(windows):
            at_edge = w == (windows - 1 if f == 0 else 0)
            cut = jnp.maximum(by_row, by_col) if at_edge else by_col
            for h in range(HEADS):
                bias[f, w, h] = (rel_bias[h] + cut * -100.0) * LOG2E
    for ref in (gq, gp, gu, gd):
        ref[...] = jnp.zeros_like(ref)

    def arrive(s):
        for copy in in_copies(s):
            copy.wait_recv()

    if steps > 1:
        pack_in(1)
    arrive(0)
    if steps > 1:
        for copy in reversed(in_copies(1)):
            copy.start()

    def step(s, carry):
        @pl.when(s + 2 < steps)
        def _():
            send_in(s + 2)

        stages, result = [], [None] * (PER * windows)
        for f in range(PER):
            at = s * PER + f
            parts = []
            for i, source in enumerate((frames, cotangent)):
                own = source[at].astype(f32)[cuts[f % 2][0], cuts[f % 2][2]]
                got = (unhalves(p[at, i]) for p in (from_side, from_row, from_corner))
                parts.append(put(f % 2, own, *got))
            for w in range(windows):
                x, c = (p[w * WS : (w + 1) * WS].reshape(wide, chan) for p in parts)
                stages.append(
                    window_block(
                        f * windows + w, x, c, bias.at[f % 2, w], gain1[...], gain2[...],
                        w_qkv, w_proj, w_up, w_down, probs, (gq, gp, gu, gd), result,
                    )
                )
        take_turns(stages)
        for f in range(PER):
            at = s * PER + f
            out = [r.reshape(WS, WS, chan) for r in result[f * windows : (f + 1) * windows]]
            out = jnp.concatenate(out, 0)
            if f % 2 == 0:
                rows_own, rows_far = slice(0, keep), slice(keep, None)
                cols_own, cols_far = slice(0, SHIFT), slice(SHIFT, None)
            else:
                rows_own, rows_far = slice(SHIFT, None), slice(0, SHIFT)
                cols_own, cols_far = slice(SHIFT, None), slice(0, SHIFT)
            back_side[at] = halves(out[rows_own, cols_far])
            back_row[at] = halves(out[rows_far, cols_own])
            back_corner[at] = halves(out[rows_far, cols_far])
            own_out[at] = halves(out[rows_own, cols_own])
        for copy in reversed(out_copies(s)):
            copy.start()

        @pl.when(s >= 2)
        def _():
            finish(s - 2)

        @pl.when(s + 1 < steps)
        def _():
            arrive(s + 1)

        return carry

    lax.fori_loop(0, steps, step, 0)

    for j in range(3):
        red[chan * j : chan * (j + 1)] = gq[:, chan * j : chan * (j + 1)]
    red[3 * chan : 4 * chan] = gp[...]
    for j in range(4):
        red[chan * (4 + j) : chan * (5 + j)] = gu[:, chan * j : chan * (j + 1)]
        red[chan * (8 + j) : chan * (9 + j)] = gd[:, chan * j : chan * (j + 1)]
    rows = red.shape[0]
    size_c = rows // 2
    size_z = size_c // (n_x * n_z)

    def copy_to(peer, src, dst, sem):
        return pltpu.make_async_remote_copy(
            src_ref=src, dst_ref=dst, send_sem=red_ssem.at[sem], recv_sem=red_rsem.at[sem],
            device_id=peer, device_id_type=MESH,
        )

    def at(start, size):
        return pl.ds(pl.multiple_of(start, 16), size)

    red_send[...] = red[...].astype(bf16)
    sem = 0
    copies = []
    base = core * size_c
    first = copy_to(core_peer(1), red_send.at[at((1 - core) * size_c, size_c)], red_core, sem)
    first.start()
    copies.append(first)
    sem += 1

    def drain_in(s, carry):
        for copy in in_copies(s):
            copy.wait_send()
        return carry

    def drain_out(s, carry):
        for copy in out_copies(s):
            copy.wait_send()
        return carry

    if steps > 1:
        finish(steps - 2)
    first.wait_recv()
    red[at(base, size_c)] += red_core[...].astype(f32)

    def reduce_stage(base, size, n, index, peer, landing, sem):
        red_send2 = red_stage[len(landings)]
        landings.append(0)
        red_send2[...] = red[at(base, size * n)].astype(bf16)
        started = []
        for s in range(1, n):
            other = lax.rem(index + s, n)
            started.append(
                copy_to(peer(s), red_send2.at[at(other * size, size)], landing.at[s - 1], sem)
            )
            started[-1].start()
            sem += 1
        base = base + index * size
        lax.fori_loop(0, nfr // PER, drain_in, 0)
        for copy in started:
            copy.wait_recv()
        total = red[at(base, size)]
        for s in range(1, n):
            total += landing[s - 1].astype(f32)
        red[at(base, size)] = total
        copies.extend(started)
        return base, sem

    landings = []
    red_stage = (full.at[pl.ds(rows, size_c)],)
    base, sem = reduce_stage(base, size_z, n_x * n_z, plane_at, plane_peer, red_plane, sem)
    red_y[y_at] = red[at(base, size_z)].astype(bf16)
    started = []
    for s in range(1, n_y):
        started.append(copy_to(y_peer(s), red_y.at[y_at], red_y.at[y_at], sem))
        started[-1].start()
        sem += 1
    finish(steps - 1)
    lax.fori_loop(0, steps, drain_out, 0)
    for copy in started:
        copy.wait_recv()
    copies.extend(started)
    total = red_y[0].astype(f32)
    for j in range(1, n_y):
        total += red_y[j].astype(f32)
    full[at(base, size_z)] = total.astype(bf16)

    def gather_stage(base, size, n, peer, sem):
        started = []
        for s in range(1, n):
            part = full.at[at(base, size)]
            started.append(copy_to(peer(s), part, part, sem))
            started[-1].start()
            sem += 1
        while copies:
            copies.pop().wait_send()
        for copy in started:
            copy.wait_recv()
        copies.extend(started)
        return sem

    sem = gather_stage(base, size_z, n_x * n_z, plane_peer, sem)
    sem = gather_stage(core * size_c, size_c, 2, core_peer, sem)
    full_out[...] = full[:rows]
    for copy in copies:
        copy.wait_send()

    def drain(s, carry):
        grad_copy(s).wait()
        return carry

    lax.fori_loop(0, steps, drain, 0)


def finish_kernel(
    factor, grad_b, full_in, grad, qkv_out, proj_out, up_out, down_out,
    narrow, wide, full, g_qkv, g_proj, g_up, g_down, load_sem, store_sem, full_sem, sum_sem,
):
    steps = load_sem.shape[0]
    per = narrow.shape[0] // steps
    chan = full.shape[1]

    def load(s):
        span = pl.ds(s * per, per)
        return pltpu.make_async_copy(grad_b.at[span], narrow.at[span], load_sem.at[s])

    def store(s):
        span = pl.ds(s * per, per)
        return pltpu.make_async_copy(wide.at[span], grad.at[span], store_sem.at[s])

    def block(j):
        return full[chan * j : chan * (j + 1)].astype(f32) * factor

    full_load = pltpu.make_async_copy(full_in, full, full_sem)
    for s in range(steps):
        load(s).start()
    full_load.start()
    for s in range(steps):
        load(s).wait()
        wide[per * s : per * (s + 1)] = narrow[per * s : per * (s + 1)].astype(f32)
        store(s).start()
    full_load.wait()
    for j in range(g_qkv.shape[1] // chan):
        g_qkv[:, chan * j : chan * (j + 1)] = block(j)
    g_proj[...] = block(3)
    for j in range(g_up.shape[1] // chan):
        g_up[:, chan * j : chan * (j + 1)] = block(4 + j)
        g_down[chan * j : chan * (j + 1)] = block(8 + j).T
    pairs = ((g_qkv, qkv_out), (g_proj, proj_out), (g_up, up_out), (g_down, down_out))
    sums = [pltpu.make_async_copy(a, b, sum_sem.at[i]) for i, (a, b) in enumerate(pairs)]
    for copy in sums:
        copy.start()
    for s in range(steps):
        store(s).wait()
    for copy in sums:
        copy.wait()


def solution(mesh):
    n_row, n_col = mesh.shape["row"], mesh.shape["col"]

    def shards(frames, cotangent, gain1, w_qkv, rel_bias, w_proj, gain2, w_up, w_down):
        nfr, tile_h, tile_w, chan = frames.shape
        ff = w_up.shape[1]
        factor = float(nfr * tile_h * tile_w * n_row * n_col) ** -0.5
        long, short = (tile_h - SHIFT) // 2, SHIFT // 2
        wide = WS * WS
        rows = 4 * chan + 2 * ff
        n_z, n_x = min(4, n_row), min(4, n_col // 2)
        n_y = (n_row // n_z) * (n_col // (2 * n_x))
        size_c = rows // 2
        size_z = size_c // (n_x * n_z)
        n_sem = 2 + 2 * (n_x * n_z - 1) + (n_y - 1)

        def pieces(k):
            sizes = (long, short, short)
            lead = (nfr,) if k == 1 else (nfr, k)
            return [pltpu.VMEM(lead + (n, 2 * SHIFT, chan), bf16) for n in sizes]

        vmem = pl.BlockSpec(memory_space=pltpu.VMEM)
        hbm = pl.BlockSpec(memory_space=pl.ANY)
        steps, windows = nfr // PER, tile_h // WS
        grad_b, full = pl.pallas_call(
            functools.partial(block_kernel, n_row, n_col),
            out_shape=[
                jax.ShapeDtypeStruct(frames.shape, bf16),
                jax.ShapeDtypeStruct((rows, chan), bf16),
            ],
            in_specs=[hbm, hbm, vmem, vmem, hbm, vmem, vmem, vmem, vmem],
            out_specs=[hbm, vmem],
            scratch_shapes=[
                pltpu.VMEM(frames.shape, bf16),
                pltpu.VMEM(frames.shape, bf16),
                pltpu.VMEM(rel_bias.shape, f32),
            ]
            + pieces(2) + pieces(2) + pieces(1) + pieces(1)
            + [
                pltpu.VMEM((nfr, long, 2 * SHIFT, chan), bf16),
                pltpu.VMEM(frames.shape, bf16),
                pltpu.VMEM((PER * windows, HEADS, wide, wide), bf16),
                pltpu.VMEM((2, windows, HEADS, wide, wide), f32),
                pltpu.VMEM((chan, 3 * chan), f32),
                pltpu.VMEM((chan, chan), f32),
                pltpu.VMEM((chan, ff), f32),
                pltpu.VMEM((chan, ff), f32),
                pltpu.VMEM((rows, chan), f32),
                pltpu.VMEM((rows, chan), bf16),
                pltpu.VMEM((size_c, chan), bf16),
                pltpu.VMEM((n_x * n_z - 1, size_z, chan), bf16),
                pltpu.VMEM((n_y, size_z, chan), bf16),
                pltpu.VMEM((rows + size_c, chan), bf16),
                pltpu.SemaphoreType.DMA((2, steps + 1)),
                pltpu.SemaphoreType.DMA((3, nfr)),
                pltpu.SemaphoreType.DMA((3, nfr)),
                pltpu.SemaphoreType.DMA((3, nfr)),
                pltpu.SemaphoreType.DMA((3, nfr)),
                pltpu.SemaphoreType.DMA((steps,)),
                pltpu.SemaphoreType.DMA((n_sem,)),
                pltpu.SemaphoreType.DMA((n_sem,)),
            ],
            compiler_params=pltpu.CompilerParams(
                collective_id=0, has_side_effects=True, vmem_limit_bytes=56 * 2**20
            ),
        )(
            frames, cotangent, gain1.reshape(1, chan), w_qkv, rel_bias, w_proj,
            gain2.reshape(1, chan), w_up, w_down,
        )

        sizes = [(chan, 3 * chan), (chan, chan), (chan, ff), (ff, chan)]
        return pl.pallas_call(
            functools.partial(finish_kernel, factor),
            out_shape=[jax.ShapeDtypeStruct(frames.shape, f32)]
            + [jax.ShapeDtypeStruct(size, f32) for size in sizes],
            in_specs=[hbm, hbm],
            out_specs=[hbm] * 5,
            scratch_shapes=[
                pltpu.VMEM(frames.shape, bf16),
                pltpu.VMEM(frames.shape, f32),
                pltpu.VMEM((rows, chan), bf16),
            ]
            + [pltpu.VMEM(size, f32) for size in sizes]
            + [
                pltpu.SemaphoreType.DMA((nfr // 2,)),
                pltpu.SemaphoreType.DMA((nfr // 2,)),
                pltpu.SemaphoreType.DMA,
                pltpu.SemaphoreType.DMA((4,)),
            ],
            compiler_params=pltpu.CompilerParams(vmem_limit_bytes=56 * 2**20),
        )(grad_b, full)

    tiles = P(None, "row", "col", None)
    return jax.shard_map(
        shards,
        mesh=mesh,
        in_specs=(tiles, tiles) + (P(),) * 7,
        out_specs=(tiles, P(), P(), P(), P()),
        check_vma=False,
    )
```
